32 devices in a mesh: dp: 16 (over z, y, x), fsdp: 2 (over core).
Axes of the slice: x: 2, y: 2, z: 4, core: 2. Of those that a mesh axis runs over, the one named last changes fastest.
Arguments:
- tokens: bfloat16 [2, 2, 5024, 768], P('fsdp', None, 'dp'), may hold values from -6 to 6
- gain_attn: bfloat16 [768], P(('dp', 'fsdp')), may hold values from 0.099609375 to 1.8984375
- gain_mlp: bfloat16 [768], P(('dp', 'fsdp')), may hold values from 0.099609375 to 1.8984375
- w_qkv: bfloat16 [768, 2304], P(('dp', 'fsdp')), may hold values from -0.21875 to 0.21875
- w_out: bfloat16 [768, 768], P(('dp', 'fsdp')), may hold values from -0.875 to 0.875
- w_up: bfloat16 [768, 3072], P(('dp', 'fsdp')), may hold values from -0.21875 to 0.21875
- w_down: bfloat16 [3072, 768], P(('dp', 'fsdp')), may hold values from -0.109375 to 0.109375
- w_dec: bfloat16 [768, 384], P(('dp', 'fsdp')), may hold values from -0.21875 to 0.21875
- mask_token: bfloat16 [384], replicated, may hold values from -6 to 6
- clip_lengths: int32 [2, 2, 64], P('fsdp'), may hold values from 0 to 314, as said below
- vis_index: int32 [2, 2, 5024], P('fsdp', None, 'dp'), may hold values from 0 to 3135, as said below
- pos_index: int32 [2, 2, 50176], P('fsdp', None, 'dp'), may hold values from 0 to 1567, as said below
- cotangent: bfloat16 [2, 2, 50176, 384], P('fsdp', None, 'dp'), may hold values from -6 to 6
Outputs:
- decoder_rows: bfloat16 [2, 2, 50176, 384], P('fsdp', None, 'dp')
- token_grad: bfloat16 [2, 2, 5024, 768], P('fsdp', None, 'dp')
- gain_attn_grad: float32 [768], P(('dp', 'fsdp'))
- gain_mlp_grad: float32 [768], P(('dp', 'fsdp'))
- qkv_grad: float32 [768, 2304], P(('dp', 'fsdp'))
- out_grad: float32 [768, 768], P(('dp', 'fsdp'))
- up_grad: float32 [768, 3072], P(('dp', 'fsdp'))
- down_grad: float32 [3072, 768], P(('dp', 'fsdp'))
- dec_grad: float32 [768, 384], P(('dp', 'fsdp'))
- mask_grad: float32 [384], replicated
The draws below stay inside these ranges and needn't reach their ends.
Inputs may be any that keep to these rules, and one draw needn't show every extreme that they name: `clip_lengths`: each device's 4 slots hold either one clip of 314 and zeros, or clips of 157 followed by clips of 78 followed by zeros, summing to at most 314; in each group and micro-batch some device holds a clip of 314. `vis_index`: the rows of a clip rise and are distinct and below 784 * (length // 78); padding rows hold 0. `pos_index`: rows past a device's clips hold 0.
All inputs are finite; a program needn't handle non-finite values.
Results may differ from the reference program's by a relative error of at most 0.013.
Values may be sent and summed in bfloat16 or wider, within the bound.
A program may use at most 192 MiB of HBM per device.

```python
import math
import jax
import jax.numpy as jnp
from jax import lax

D = 768
HEADS = 12
HEAD = 64
FF = 3072
DD = 384
SHORT = 78
MID = 157
LONG = 314
SPATIAL = 196
MICRO = 2
CLIPS = 4
FULL_UNIT = 784
GROUPS = 2
ROWS = 5024
FULL_ROWS = 50176
N_DP = 16


def clip_table(key):
    split_keys = jax.random.split(jax.random.fold_in(key, 101), 4)
    grid_shape = (GROUPS, MICRO, N_DP)
    long_kind = jax.random.randint(split_keys[0], grid_shape, 0, 3) == 0
    forced = jax.random.randint(split_keys[1], (GROUPS, MICRO, 1), 0, N_DP)
    long_kind = long_kind | (jnp.arange(N_DP)[None, None, :] == forced)
    mid_count = jax.random.randint(split_keys[2], grid_shape, 0, 3)
    room_left = (LONG - mid_count * MID) // SHORT
    short_count = jnp.maximum(room_left - jax.random.randint(split_keys[3], grid_shape, 0, 3), 0)
    slot_ids = jnp.arange(CLIPS)[None, None, None, :]
    regular = jnp.where(slot_ids < mid_count[..., None], MID, jnp.where(slot_ids < (mid_count + short_count)[..., None], SHORT, 0))
    single = jnp.where(slot_ids == 0, LONG, 0)
    return jnp.where(long_kind[..., None], single, regular).astype(jnp.int32)


def draw_clip_lengths(key, part):
    return clip_table(key).reshape(GROUPS, MICRO, N_DP * CLIPS)


def draw_vis_index(key, part):
    lengths = clip_table(key)
    key = jax.random.fold_in(key, 2)
    span = 4 * FULL_UNIT
    full_sizes = lengths // SHORT * FULL_UNIT
    spot_ids = jnp.arange(span)
    scores = jax.random.randint(key, lengths.shape + (span,), 0, 2 ** 18)
    scores = jnp.where(spot_ids < full_sizes[..., None], scores * span + spot_ids, 2 ** 30)
    rank_ids = jnp.argsort(jnp.argsort(scores, axis=-1), axis=-1)
    chosen = jnp.sort(jnp.where(rank_ids < lengths[..., None], spot_ids, span), axis=-1)
    clip_ends = jnp.cumsum(lengths, axis=-1)
    clip_starts = clip_ends - lengths
    row_ids = jnp.arange(LONG)
    clip_of = jnp.sum((row_ids[:, None] >= clip_ends[..., None, :]).astype(jnp.int32), axis=-1)
    clip_safe = jnp.minimum(clip_of, CLIPS - 1)
    within = jnp.minimum(row_ids - jnp.take_along_axis(clip_starts, clip_safe, axis=-1), span - 1)
    flat_chosen = chosen.reshape(lengths.shape[:-1] + (CLIPS * span,))
    picked = jnp.take_along_axis(flat_chosen, clip_safe * span + within, axis=-1)
    result = jnp.where(clip_of < CLIPS, picked, 0)
    return result.reshape(GROUPS, MICRO, N_DP * LONG).astype(jnp.int32)


def draw_pos_index(key, part):
    lengths = clip_table(key)
    key = jax.random.fold_in(key, 3)
    shifts = jax.random.randint(key, lengths.shape, 0, 8)
    ratio = lengths // SHORT
    full_sizes = ratio * FULL_UNIT
    full_ends = jnp.cumsum(full_sizes, axis=-1)
    full_starts = full_ends - full_sizes
    row_ids = jnp.arange(4 * FULL_UNIT)
    clip_of = jnp.sum((row_ids[:, None] >= full_ends[..., None, :]).astype(jnp.int32), axis=-1)
    clip_safe = jnp.minimum(clip_of, CLIPS - 1)
    within = row_ids - jnp.take_along_axis(full_starts, clip_safe, axis=-1)
    rate_of = jnp.maximum(jnp.take_along_axis(ratio, clip_safe, axis=-1), 1)
    shift_of = jnp.take_along_axis(shifts, clip_safe, axis=-1)
    frame = (within // SPATIAL * 2 // rate_of + shift_of) % 8
    result = jnp.where(clip_of < CLIPS, frame * SPATIAL + within % SPATIAL, 0)
    return result.reshape(GROUPS, MICRO, N_DP * 4 * FULL_UNIT).astype(jnp.int32)


def block_scale(own_key, dims, cuts, low, largest):
    loudness = 1.0
    for dim, shards_of in cuts:
        draws = jax.random.uniform(jax.random.fold_in(jax.random.fold_in(own_key, 6), dim), (shards_of,), jnp.float32, low / len(cuts), largest / len(cuts))
        loudness = loudness * jnp.repeat(jnp.exp(draws), dims[dim] // shards_of).reshape((-1,) + (1,) * (len(dims) - 1 - dim))
    return loudness


def centred(key, dims, width, limit, pieces=(), dtype=jnp.bfloat16):
    array = width * jax.random.normal(key, dims, jnp.float32)
    if pieces:
        array = array * block_scale(key, dims, pieces, -0.22, 0.18)
    return jnp.clip(array, -limit, limit).astype(dtype)


def setup_inputs(seed: int = 0) -> dict:
    seeds = jax.random.split(jax.random.key(seed), 14)
    return {
        "tokens": centred(seeds[0], (GROUPS, MICRO, ROWS, D), 1.0, 6.0, ((0, 2), (2, 16))),
        "gain_attn": jnp.clip(1.0 + 0.18 * jax.random.normal(seeds[1], (D,), jnp.float32), 0.099609375, 1.8984375).astype(jnp.bfloat16),
        "gain_mlp": jnp.clip(1.0 + 0.18 * jax.random.normal(seeds[2], (D,), jnp.float32), 0.099609375, 1.8984375).astype(jnp.bfloat16),
        "w_qkv": centred(seeds[3], (D, 3 * D), D ** -0.5, 0.21875, ((0, 32),)),
        "w_out": centred(seeds[4], (D, D), (D // 16) ** -0.5, 0.875, ((0, 32),)),
        "w_up": centred(seeds[5], (D, FF), D ** -0.5, 0.21875, ((0, 32),)),
        "w_down": centred(seeds[6], (FF, D), FF ** -0.5, 0.109375, ((0, 32),)),
        "w_dec": centred(seeds[7], (D, DD), D ** -0.5, 0.21875, ((0, 32),)),
        "mask_token": centred(seeds[8], (DD,), 1.0, 6.0),
        "clip_lengths": draw_clip_lengths(jax.random.fold_in(seeds[13], 71), 0),
        "vis_index": draw_vis_index(jax.random.fold_in(seeds[13], 71), 0),
        "pos_index": draw_pos_index(jax.random.fold_in(seeds[13], 71), 0),
        "cotangent": centred(seeds[12], (GROUPS, MICRO, FULL_ROWS, DD), 1.0, 6.0, ((0, 2), (2, 16))),
    }


@jax.custom_vjp
def low(v):
    return lax.optimization_barrier(v.astype(jnp.bfloat16)).astype(jnp.float32)

@jax.custom_vjp
def low_back(v):
    return v

def low_keep(v):
    return (low(v), None)

def low_pass(kept, grad):
    return (grad,)

def back_keep(v):
    return (v, None)

def back_low(kept, grad):
    return (low(grad),)
low.defvjp(low_keep, low_pass)
low_back.defvjp(back_keep, back_low)
NEG = -1e+30
EPS = 1e-06
PRECISE = lax.Precision.HIGHEST

def layer_norm(values, scale_gain):
    center = values - lax.optimization_barrier(jnp.mean(values, axis=-1, keepdims=True))
    spread = lax.optimization_barrier(jnp.mean(center * center, axis=-1, keepdims=True))
    return center * lax.rsqrt(spread + EPS) * scale_gain

def softmax_rows(scores):
    shifted = scores - lax.optimization_barrier(jnp.max(scores, axis=-1, keepdims=True))
    powers = jnp.exp(shifted)
    return powers / lax.optimization_barrier(jnp.sum(powers, axis=-1, keepdims=True))

def gelu_exact(values):
    return 0.5 * values * (1.0 + lax.erf(values * (1.0 / math.sqrt(2.0))))

def sinusoid(table_index, features):
    channel = jnp.arange(features)
    rates = jnp.exp((channel // 2 * 2).astype(jnp.float32) * (-math.log(10000.0) / features))
    angles = table_index.astype(jnp.float32)[:, None] * rates[None, :]
    return jnp.where(channel % 2 == 0, jnp.sin(angles), jnp.cos(angles))

def block_layout(lengths, row_count):
    clip_ends = jnp.cumsum(lengths).astype(jnp.int32)
    full_sizes = (lengths // SHORT * FULL_UNIT).astype(jnp.int32)
    full_ends = jnp.cumsum(full_sizes).astype(jnp.int32)
    full_starts = full_ends - full_sizes
    row_ids = jnp.arange(row_count)
    clip_of = lax.optimization_barrier(jnp.sum((row_ids[:, None] >= clip_ends[None, :]).astype(jnp.int32), axis=1)).astype(jnp.int32)
    live_rows = clip_of < lengths.shape[0]
    slot_ids = jnp.arange(lengths.shape[0])
    start_of = lax.optimization_barrier(jnp.sum(jnp.where(clip_of[:, None] == slot_ids[None, :], full_starts[None, :], 0), axis=1)).astype(jnp.int32)
    return (clip_of, live_rows, start_of, full_ends[-1])

def encode_block(block_in, lengths, visible, position, gain_first, gain_second, w_qkv, w_out, w_up, w_down, w_dec, mask_row):
    row_count = block_in.shape[0]
    clip_of, live_rows, start_of, total_full = block_layout(lengths, row_count)
    same_clip = clip_of[:, None] == clip_of[None, :]
    normed = low(layer_norm(block_in, gain_first))
    mixed_qkv = low(low_back(jnp.dot(normed, w_qkv, precision=PRECISE)))
    queries = mixed_qkv[:, :D].reshape(row_count, HEADS, HEAD)
    key_rows = mixed_qkv[:, D:2 * D].reshape(row_count, HEADS, HEAD)
    value_rows = mixed_qkv[:, 2 * D:].reshape(row_count, HEADS, HEAD)
    scores = jnp.einsum('qhd,khd->hqk', queries, key_rows, precision=PRECISE) * HEAD ** (-0.5)
    scores = low_back(jnp.where(same_clip[None], scores, NEG))
    weights = low(softmax_rows(scores))
    attended = jnp.einsum('hqk,khd->qhd', weights, value_rows, precision=PRECISE).reshape(row_count, D)
    attended = low(low_back(attended))
    after_attn = block_in + low_back(jnp.dot(attended, w_out, precision=PRECISE))
    hidden = low(layer_norm(after_attn, gain_second))
    upward = low_back(jnp.dot(hidden, w_up, precision=PRECISE))
    activated = low(gelu_exact(upward))
    after_mlp = after_attn + low_back(jnp.dot(activated, w_down, precision=PRECISE))
    projected = low(low_back(jnp.dot(low(after_mlp), w_dec, precision=PRECISE)))
    full_index = jnp.arange(4 * FULL_UNIT)
    target = start_of + visible
    place_map = ((full_index[:, None] == target[None, :]) & live_rows[None, :]).astype(jnp.float32)
    covered = lax.optimization_barrier(jnp.sum(place_map, axis=1))
    full_live = (full_index < total_full).astype(jnp.float32)
    return jnp.dot(place_map, projected, precision=PRECISE) + (full_live - covered)[:, None] * mask_row[None, :] + full_live[:, None] * sinusoid(position, DD)

def reference(tokens, gain_attn, gain_mlp, w_qkv, w_out, w_up, w_down, w_dec, mask_token, clip_lengths, vis_index, pos_index, cotangent):
    batch_count = GROUPS * MICRO
    lengths = clip_lengths.reshape(batch_count, N_DP, CLIPS)
    totals = lax.optimization_barrier(jnp.sum(lengths, axis=2)).astype(jnp.int32)
    offsets = (jnp.cumsum(totals, axis=1) - totals).astype(jnp.int32)
    row_ids = jnp.arange(LONG)
    stream = offsets[:, :, None] + row_ids[None, None, :]
    live_rows = row_ids[None, None, :] < totals[:, :, None]
    source_rows = jnp.where(live_rows, stream % N_DP * LONG + stream // N_DP, 0).astype(jnp.int32)

    def forward(tokens_f, gain_first, gain_second, qkv_f, out_f, up_f, down_f, dec_f, mask_f):
        flat_rows = tokens_f.reshape(batch_count, N_DP * LONG, D)
        blocks = jax.vmap(lambda rows_in, picks: jnp.take(rows_in, picks.reshape(-1), axis=0))(flat_rows, source_rows)
        blocks = jnp.where(live_rows.reshape(batch_count, N_DP * LONG)[..., None], blocks, 0.0)
        blocks = blocks.reshape(batch_count * N_DP, LONG, D)

        def one_block(packed):
            return encode_block(packed[0], packed[1], packed[2], packed[3], gain_first, gain_second, qkv_f, out_f, up_f, down_f, dec_f, mask_f)
        decoded = lax.map(jax.checkpoint(one_block), (blocks, lengths.reshape(-1, CLIPS), vis_index.reshape(-1, LONG), pos_index.reshape(-1, 4 * FULL_UNIT)))
        return decoded.reshape(GROUPS, MICRO, N_DP * 4 * FULL_UNIT, DD)
    inputs = tuple((item.astype(jnp.float32) for item in (tokens, gain_attn, gain_mlp, w_qkv, w_out, w_up, w_down, w_dec, mask_token)))
    decoded, pull_back = jax.vjp(forward, *inputs)
    gradients = pull_back(cotangent.astype(jnp.float32))
    return (decoded.astype(jnp.bfloat16), gradients[0].astype(jnp.bfloat16), gradients[1], gradients[2], gradients[3], gradients[4], gradients[5], gradients[6], gradients[7], gradients[8])
```

```python
import math

import jax
import jax.numpy as jnp
from jax import lax
from jax.experimental import pallas as pl
from jax.experimental.pallas import tpu as pltpu
from jax.sharding import PartitionSpec as P

HEADS = 12
HEAD = 64
SHORT = 78
FULL_UNIT = 784


NEG = -1e30
EPS = 1e-06


def layer_norm(values, scale_gain):
    center = values - jnp.mean(values, axis=-1, keepdims=True)
    spread = jnp.mean(center * center, axis=-1, keepdims=True)
    return center * lax.rsqrt(spread + EPS) * scale_gain


def softmax_rows(scores):
    shifted = scores - jnp.max(scores, axis=-1, keepdims=True)
    powers = jnp.exp(shifted)
    return powers / jnp.sum(powers, axis=-1, keepdims=True)


def gelu_exact(values):
    return 0.5 * values * (1.0 + lax.erf(values * (1.0 / math.sqrt(2.0))))


def sinusoid(table_index, features):
    channel = jnp.arange(features)
    rates = jnp.exp((channel // 2 * 2).astype(jnp.float32) * (-math.log(10000.0) / features))
    angles = table_index.astype(jnp.float32)[:, None] * rates[None, :]
    return jnp.where(channel % 2 == 0, jnp.sin(angles), jnp.cos(angles))


def block_layout(lengths, row_count):
    clip_ends = jnp.cumsum(lengths)
    full_sizes = lengths // SHORT * FULL_UNIT
    full_ends = jnp.cumsum(full_sizes)
    full_starts = full_ends - full_sizes
    row_ids = jnp.arange(row_count)
    clip_of = jnp.sum((row_ids[:, None] >= clip_ends[None, :]).astype(jnp.int32), axis=1)
    live_rows = clip_of < lengths.shape[0]
    slot_ids = jnp.arange(lengths.shape[0])
    start_of = jnp.sum(
        jnp.where(clip_of[:, None] == slot_ids[None, :], full_starts[None, :], 0), axis=1
    )
    return (clip_of, live_rows, start_of, full_ends[-1])


def contract(left_side, right_side, pattern):
    return jnp.einsum(pattern, left_side, right_side, preferred_element_type=jnp.float32)


def layer_pass(block_in, lengths, visible, position, grad_rows, params, mask_token):
    gain_attn, gain_mlp, w_qkv, w_out, w_up, w_down, w_dec = params
    row_count = block_in.shape[0]
    features = block_in.shape[1]
    full_count = grad_rows.shape[0]
    clip_of, live_rows, start_of, total_full = block_layout(lengths, row_count)
    same_clip = clip_of[:, None] == clip_of[None, :]
    inputs = block_in.astype(jnp.float32)
    normed, norm_attn_back = jax.vjp(layer_norm, inputs, gain_attn.astype(jnp.float32))
    normed = normed.astype(jnp.bfloat16)
    mixed_qkv = contract(normed, w_qkv, "pc,ce->pe").astype(jnp.bfloat16)
    queries = mixed_qkv[:, :features].reshape(row_count, HEADS, HEAD)
    key_rows = mixed_qkv[:, features : 2 * features].reshape(row_count, HEADS, HEAD)
    value_rows = mixed_qkv[:, 2 * features :].reshape(row_count, HEADS, HEAD)
    scores = contract(queries, key_rows, "qhd,khd->hqk") * HEAD ** (-0.5)
    scores = jnp.where(same_clip[None], scores, NEG)
    weights, soft_back = jax.vjp(softmax_rows, scores)
    weights_low = weights.astype(jnp.bfloat16)
    attended = (
        contract(weights_low, value_rows, "hqk,khd->qhd")
        .reshape(row_count, features)
        .astype(jnp.bfloat16)
    )
    after_attn = inputs + contract(attended, w_out, "pc,ce->pe")
    hidden, norm_mlp_back = jax.vjp(layer_norm, after_attn, gain_mlp.astype(jnp.float32))
    hidden = hidden.astype(jnp.bfloat16)
    upward = contract(hidden, w_up, "pc,cf->pf")
    activated, gelu_back = jax.vjp(gelu_exact, upward)
    activated = activated.astype(jnp.bfloat16)
    after_mlp = after_attn + contract(activated, w_down, "pf,fc->pc")
    final_low = after_mlp.astype(jnp.bfloat16)
    projected = contract(final_low, w_dec, "pc,ce->pe").astype(jnp.bfloat16)
    full_index = jnp.arange(full_count)
    target = start_of + visible
    place_map = ((full_index[:, None] == target[None, :]) & live_rows[None, :]).astype(jnp.bfloat16)
    covered = jnp.sum(place_map, axis=1, dtype=jnp.float32)
    full_live = (full_index < total_full).astype(jnp.float32)
    masked_share = full_live - covered
    decoded = (
        contract(place_map, projected, "ip,pe->ie")
        + masked_share[:, None] * mask_token.astype(jnp.float32)[None, :]
        + full_live[:, None] * sinusoid(position, projected.shape[1])
    )
    grad_full = grad_rows.astype(jnp.float32)
    mask_term = jnp.sum(masked_share[:, None] * grad_full, axis=0)
    back_proj = contract(place_map, grad_rows, "ip,ie->pe").astype(jnp.bfloat16)
    grad_dec = contract(final_low, back_proj, "pc,pe->ce")
    back_final = contract(back_proj, w_dec, "pe,ce->pc")
    back_mlp = back_final.astype(jnp.bfloat16)
    grad_down = contract(activated, back_mlp, "pf,pc->fc")
    back_act = contract(back_mlp, w_down, "pc,fc->pf")
    back_up = gelu_back(back_act)[0].astype(jnp.bfloat16)
    grad_up = contract(hidden, back_up, "pc,pf->cf")
    back_hidden = contract(back_up, w_up, "pf,cf->pc")
    back_norm_mlp, grad_gain_mlp = norm_mlp_back(back_hidden)
    back_after = back_final + back_norm_mlp
    back_attn_out = back_after.astype(jnp.bfloat16)
    grad_out = contract(attended, back_attn_out, "pc,pe->ce")
    back_attended = (
        contract(back_attn_out, w_out, "pe,ce->pc")
        .astype(jnp.bfloat16)
        .reshape(row_count, HEADS, HEAD)
    )
    back_weights = contract(back_attended, value_rows, "qhd,khd->hqk")
    back_values = contract(weights_low, back_attended, "hqk,qhd->khd")
    back_scores = soft_back(back_weights)[0].astype(jnp.bfloat16) * HEAD ** (-0.5)
    back_queries = contract(back_scores, key_rows, "hqk,khd->qhd")
    back_keys = contract(back_scores, queries, "hqk,qhd->khd")
    back_mixed = jnp.concatenate(
        [
            back_queries.reshape(row_count, features),
            back_keys.reshape(row_count, features),
            back_values.reshape(row_count, features),
        ],
        axis=1,
    ).astype(jnp.bfloat16)
    grad_qkv = contract(normed, back_mixed, "pc,pe->ce")
    back_normed = contract(back_mixed, w_qkv, "pe,ce->pc")
    back_inputs, grad_gain_attn = norm_attn_back(back_normed)
    back_block = (back_after + back_inputs).astype(jnp.bfloat16)
    gradients = (grad_gain_attn, grad_gain_mlp, grad_qkv, grad_out, grad_up, grad_down, grad_dec)
    return (decoded.astype(jnp.bfloat16), back_block, gradients, mask_term)


def per_device(
    tokens,
    gain_attn,
    gain_mlp,
    w_qkv,
    w_out,
    w_up,
    w_down,
    w_dec,
    mask_token,
    clip_lengths,
    vis_index,
    pos_index,
    cotangent,
):
    shards = (gain_attn, gain_mlp, w_qkv, w_out, w_up, w_down, w_dec)
    spread = lax.axis_size(("dp", "fsdp"))
    running = tuple(
        (jnp.zeros((piece.shape[0] * spread,) + piece.shape[1:], jnp.float32) for piece in shards)
    )
    devices = lax.axis_size("dp")
    device = lax.axis_index("dp")
    micro_count = tokens.shape[1]
    row_count = tokens.shape[2]
    features = tokens.shape[3]
    slot_count = -(-row_count // devices)
    mask_sum = jnp.zeros(mask_token.shape, jnp.float32)
    decoded_all = []
    returned_all = []
    for micro_step in range(micro_count):
        params = (
            lax.all_gather(shards[0], ("dp", "fsdp"), axis=0, tiled=True),
            lax.all_gather(shards[1], ("dp", "fsdp"), axis=0, tiled=True),
            lax.all_gather(shards[2], ("dp", "fsdp"), axis=0, tiled=True),
            lax.all_gather(shards[3], ("dp", "fsdp"), axis=0, tiled=True),
            lax.all_gather(shards[4], ("dp", "fsdp"), axis=0, tiled=True),
            lax.all_gather(shards[5], ("dp", "fsdp"), axis=0, tiled=True),
            lax.all_gather(shards[6], ("dp", "fsdp"), axis=0, tiled=True),
        )
        lengths = clip_lengths[0, micro_step].reshape(devices, -1)
        filled = jnp.sum(lengths, axis=1)
        offsets = jnp.cumsum(filled) - filled
        leading = (device - offsets) % devices
        first_row = (offsets + leading) // devices
        slot_index = jnp.arange(slot_count)
        sent_live = leading[None, :] + slot_index[:, None] * devices < filled[None, :]
        pick_rows = jnp.where(sent_live, first_row[None, :] + slot_index[:, None], row_count)
        source_rows = jnp.concatenate(
            [tokens[0, micro_step], jnp.zeros((1, features), tokens.dtype)], axis=0
        )
        outgoing = jnp.take(source_rows, pick_rows, axis=0)
        incoming = lax.all_to_all(outgoing, "dp", split_axis=1, concat_axis=1, tiled=True)
        own_offset = lax.dynamic_index_in_dim(offsets, device, 0, keepdims=False)
        block_in = jnp.roll(incoming, -own_offset, axis=1).reshape(slot_count * devices, features)[
            :row_count
        ]
        own_lengths = lax.dynamic_index_in_dim(lengths, device, 0, keepdims=False)
        decoded, back_block, gradients, mask_term = layer_pass(
            block_in,
            own_lengths,
            vis_index[0, micro_step],
            pos_index[0, micro_step],
            cotangent[0, micro_step],
            params,
            mask_token,
        )
        running = tuple(
            (total_piece + new_piece for total_piece, new_piece in zip(running, gradients))
        )
        mask_sum = mask_sum + mask_term
        padded_back = jnp.concatenate(
            [back_block, jnp.zeros((slot_count * devices - row_count, features), jnp.bfloat16)],
            axis=0,
        )
        outgoing_back = jnp.roll(
            padded_back.reshape(slot_count, devices, features), own_offset, axis=1
        )
        incoming_back = lax.all_to_all(outgoing_back, "dp", split_axis=1, concat_axis=1, tiled=True)
        returned = (
            jnp.zeros((row_count + 1, features), jnp.bfloat16)
            .at[pick_rows]
            .add(incoming_back)[:row_count]
        )
        decoded_all.append(decoded)
        returned_all.append(returned)
    shares = (
        lax.psum_scatter(running[0], ("dp", "fsdp"), scatter_dimension=0, tiled=True),
        lax.psum_scatter(running[1], ("dp", "fsdp"), scatter_dimension=0, tiled=True),
        lax.psum_scatter(running[2], ("dp", "fsdp"), scatter_dimension=0, tiled=True),
        lax.psum_scatter(running[3], ("dp", "fsdp"), scatter_dimension=0, tiled=True),
        lax.psum_scatter(running[4], ("dp", "fsdp"), scatter_dimension=0, tiled=True),
        lax.psum_scatter(running[5], ("dp", "fsdp"), scatter_dimension=0, tiled=True),
        lax.psum_scatter(running[6], ("dp", "fsdp"), scatter_dimension=0, tiled=True),
    )
    mask_grad = lax.psum(mask_sum, ("dp", "fsdp"))
    return (
        jnp.stack(decoded_all)[None],
        jnp.stack(returned_all)[None],
        shares[0],
        shares[1],
        shares[2],
        shares[3],
        shares[4],
        shares[5],
        shares[6],
        mask_grad,
    )


BF = jnp.bfloat16
F32 = jnp.float32
MESH = pl.DeviceIdType.MESH
MICROS = 2
RP = 320
RT = MICROS * RP
D = 768
DD = 384
FULL = 3136
SLOT = 24
PAIR = MICROS * SLOT
NZ, NY, NX = 4, 2, 2
CHIPS = NZ * NY * NX
CH = 48
C_QKV, C_DEC, C_OUT, C_UP, C_DOWN, C_ALL = 0, 1152, 1408, 1792, 3328, 4864
SWAPPED = C_DOWN
GATHERS = ((C_QKV, 768, 1408), (C_OUT, 896, 1920), (C_DOWN, 768, 1536))
DOWN, DEC, UP, OUT, QKV = range(5)
WIDTH = (1536, 256, 1536, 384, 1152)
FIRST = (768, 128, 768, 128, 640)
PLACE = (0, C_DEC, C_UP, C_OUT, C_QKV)
YC = 448
EC = 224


def _nn(a, b):
    return lax.dot_general(a, b, (((1,), (0,)), ((), ())), preferred_element_type=F32)


def _nt(a, b):
    return lax.dot_general(a, b, (((1,), (1,)), ((), ())), preferred_element_type=F32)


def _tn(a, b):
    return lax.dot_general(a, b, (((0,), (0,)), ((), ())), preferred_element_type=F32)


def _iota(shape, dim):
    return lax.broadcasted_iota(jnp.int32, shape, dim)


def _mega(
    tok, wsw, wdn, mask_tok, lens, vis, pos, cot,
    o_dec, o_tok, o_cat, o_dn, o_vec,
    W, gD, big, X, A, Tb, Q, O, X1, H, G, GP, X2, dZ, dX, dW, Zx, outg, inc, incb, bias, tab,
    swp, stg, r3, r4, fin, vec, rv,
    h0, h1a, h1b, h2a, h2b,
    yk, swk, agz, ag1, ag2, ag3, a2, a2b, rs0, rs1, rs2, rs3, rs4, rvk, lk, ok, tk,
):
    dp = lax.axis_index("dp")
    f = lax.axis_index("fsdp")
    x = lax.rem(dp, 2)
    y = lax.rem(lax.div(dp, 2), 2)
    z = lax.div(dp, 4)
    sib = (dp, 1 - f)
    xn = (dp + 1 - 2 * x, f)
    yn = (dp + 2 - 4 * y, f)

    def zpeer(k):
        return lax.rem(z + k, NZ)

    def dev_z(k):
        return (lax.rem(dp + 4 * k, CHIPS), f)

    def peer(k):
        return (lax.rem(dp + k, CHIPS), f)

    def remote(src, dst, sems, idx, dev):
        return pltpu.make_async_remote_copy(
            src_ref=src, dst_ref=dst, send_sem=sems.at[(0,) + idx], recv_sem=sems.at[(1,) + idx],
            device_id=dev, device_id_type=MESH,
        )

    bar = pltpu.get_barrier_semaphore()
    pl.semaphore_signal(bar, inc=1, device_id=sib, device_id_type=MESH)
    for k in range(1, CHIPS):
        pl.semaphore_signal(bar, inc=1, device_id=peer(k), device_id_type=MESH)
    pl.semaphore_wait(bar, CHIPS)

    swap = remote(wsw.at[1 - f], swp, swk, (0,), sib)
    swap.start()
    y_load = [pltpu.make_async_copy(cot.at[m], big.at[pl.ds(m * FULL, FULL)], yk.at[m]) for m in range(MICROS)]
    tok_load = pltpu.make_async_copy(tok, A, tk.at[0])
    tok_load.start()
    for c in y_load:
        c.start()

    def ag_start(g):
        c0, _, n = GATHERS[g]
        cps = []
        for k in range(1, NZ):
            part = W.at[f, z, y, x, :, c0 : c0 + n]
            cps.append(remote(part, part, agz, (g, k - 1), dev_z(k)))
            cps[-1].start()
        return cps

    def ag_1(g):
        c0, a, n = GATHERS[g]
        pa = W.at[f, :, y, x, :, c0 : c0 + a]
        pb = W.at[f, :, y, x, :, c0 + a : c0 + n]
        cps = [remote(pa, pa, ag1, (g, 0), yn), remote(pb, pb, ag1, (g, 1), xn)]
        for c in cps:
            c.start()
        return cps

    def ag_2(g):
        c0, a, n = GATHERS[g]
        pa = W.at[f, :, :, x, :, c0 : c0 + a]
        pb = W.at[f, :, y, :, :, c0 + a : c0 + n]
        cps = [remote(pa, pa, ag2, (g, 0), xn), remote(pb, pb, ag2, (g, 1), yn)]
        for c in cps:
            c.start()
        return cps

    def ag_3(g):
        c0, _, n = GATHERS[g]
        part = W.at[f, :, :, :, :, c0 : c0 + n]
        cp = remote(part, part, ag3, (g,), sib)
        cp.start()
        return [cp]

    ag_flight = {}
    ag_steps = (ag_start, ag_1, ag_2, ag_3)

    def ag(g, step):
        if step > 0:
            for c in ag_flight[g]:
                c.wait()
        if step < 4:
            ag_flight[g] = ag_steps[step](g)

    slots = ((gD, 0), (W, C_DEC), (W, C_DOWN), (W, C_OUT), (W, C_UP))
    rs_flight = {}
    hoff = (0, 1536, 1792, 3328, 3712)
    hoa = (0, 768, 896, 1664, 1792)
    hob = (0, 768, 896, 1664, 1920)

    def rs_a(g):
        ref, c0 = slots[g]
        w = WIDTH[g]
        cp = remote(ref.at[1 - f, :, :, :, :, c0 : c0 + w], h0.at[:, :, :, :, hoff[g] : hoff[g] + w], rs0, (g,), sib)
        cp.start()
        rs_flight[g] = [cp]

    def staged(sources, adds):
        cps = []
        for i, (src, dst) in enumerate(sources):
            cps.append(pltpu.make_async_copy(src, dst, lk.at[i % 2]))
        cps[0].start()
        for i, c in enumerate(cps):
            if i + 1 < len(cps):
                cps[i + 1].start()
            c.wait()
            adds[i]()

    def rs_b(g):
        ref, c0 = slots[g]
        w, a = WIDTH[g], FIRST[g]
        for c in rs_flight[g]:
            c.wait()
        sources, adds = [], []
        for i in range(NZ):
            slot = stg.at[i % 2, :, :, :, 0:w]
            sources.append((h0.at[i, :, :, :, hoff[g] : hoff[g] + w], slot))

            def add(i=i, slot=slot):
                for j in range(4):
                    yy, xx = j // 2, j % 2
                    ref[f, i, yy, xx, :, c0 : c0 + w] = ref[f, i, yy, xx, :, c0 : c0 + w] + slot[yy, xx]

            adds.append(add)
        staged(sources, adds)
        cps = [
            remote(ref.at[f, :, :, 1 - x, :, c0 : c0 + a], h1a.at[:, :, :, hoa[g] : hoa[g] + a], rs1, (g, 0), xn),
            remote(ref.at[f, :, 1 - y, :, :, c0 + a : c0 + w], h1b.at[:, :, :, hob[g] : hob[g] + w - a], rs1, (g, 1), yn),
        ]
        for c in cps:
            c.start()
        rs_flight[g] = cps

    def rs_c(g):
        ref, c0 = slots[g]
        w, a = WIDTH[g], FIRST[g]
        b = w - a
        for c in rs_flight[g]:
            c.wait()
        sources, adds = [], []
        for half in range(2):
            sl = stg.at[0, :, :, :, half * 768 : half * 768 + a]
            sources.append((h1a.at[2 * half : 2 * half + 2, :, :, hoa[g] : hoa[g] + a], sl))

            def add_a(half=half, sl=sl):
                for zz in range(2):
                    for yy in range(2):
                        at = (f, 2 * half + zz, yy, x, slice(None), slice(c0, c0 + a))
                        ref[at] = ref[at] + sl[zz, yy]

            adds.append(add_a)
            sl = stg.at[1, :, :, :, half * 768 : half * 768 + b]
            sources.append((h1b.at[2 * half : 2 * half + 2, :, :, hob[g] : hob[g] + b], sl))

            def add_b(half=half, sl=sl):
                for zz in range(2):
                    for xx in range(2):
                        at = (f, 2 * half + zz, y, xx, slice(None), slice(c0 + a, c0 + w))
                        ref[at] = ref[at] + sl[zz, xx]

            adds.append(add_b)
        staged(sources, adds)
        cps = [
            remote(ref.at[f, :, 1 - y, x, :, c0 : c0 + a], h2a.at[:, :, hoa[g] : hoa[g] + a], rs2, (g, 0), yn),
            remote(ref.at[f, :, y, 1 - x, :, c0 + a : c0 + w], h2b.at[:, :, hob[g] : hob[g] + b], rs2, (g, 1), xn),
        ]
        for c in cps:
            c.start()
        rs_flight[g] = cps

    def rs_d(g):
        ref, c0 = slots[g]
        w, a = WIDTH[g], FIRST[g]
        b = w - a
        for c in rs_flight[g]:
            c.wait()
        sl_a = stg.at[0, :, :, :, 0:a]
        sl_b = stg.at[1, :, :, :, 0:b]
        sources, adds = [], []
        for half in range(2):
            sla = stg.at[0, half, :, :, 0:a]
            slb = stg.at[1, half, :, :, 0:b]
            sources.append((h2a.at[2 * half : 2 * half + 2, :, hoa[g] : hoa[g] + a], sla))
            sources.append((h2b.at[2 * half : 2 * half + 2, :, hob[g] : hob[g] + b], slb))

            def add_a(half=half, sl=sla):
                for zz in range(2):
                    at = (f, 2 * half + zz, y, x, slice(None), slice(c0, c0 + a))
                    ref[at] = ref[at] + sl[zz]

            def add_b(half=half, sl=slb):
                for zz in range(2):
                    at = (f, 2 * half + zz, y, x, slice(None), slice(c0 + a, c0 + w))
                    ref[at] = ref[at] + sl[zz]

            adds += [add_a, add_b]
        staged(sources, adds)
        cps = []
        for k in range(1, NZ):
            cps.append(
                remote(ref.at[f, zpeer(k), y, x, :, c0 : c0 + w], r3.at[k - 1, :, hoff[g] : hoff[g] + w], rs3, (g, k - 1), dev_z(k))
            )
            cps[-1].start()
        rs_flight[g] = cps

    def rs_e(g):
        ref, c0 = slots[g]
        w = WIDTH[g]
        for c in rs_flight[g]:
            c.wait()
        total = ref[f, z, y, x, :, c0 : c0 + w].astype(F32)
        for k in range(NZ - 1):
            total = total + r3[k, :, hoff[g] : hoff[g] + w].astype(F32)
        if g == DOWN:
            o_dn[...] = total
            rs_flight[g] = []
            return
        p = PLACE[g]
        fin[:, p : p + w] = total
        o_cat[f, :, p : p + w] = fin[pl.ds(pl.multiple_of(24 * f, 8), 24), p : p + w]
        cp = remote(fin.at[pl.ds(pl.multiple_of(24 * (1 - f), 8), 24), p : p + w], r4.at[:, p : p + w], rs4, (g,), sib)
        cp.start()
        rs_flight[g] = [cp]

    def rs_f(g):
        for c in rs_flight[g]:
            c.wait()
        if g != DOWN:
            p, w = PLACE[g], WIDTH[g]
            o_cat[1 - f, :, p : p + w] = r4[:, p : p + w]

    filled = [[None] * CHIPS for _ in range(MICROS)]
    before = [[None] * CHIPS for _ in range(MICROS)]
    mine = []
    own = []
    for m in range(MICROS):
        running = jnp.int32(0)
        at_me = jnp.int32(0)
        for d in range(CHIPS):
            total = lens[m, 4 * d] + lens[m, 4 * d + 1] + lens[m, 4 * d + 2] + lens[m, 4 * d + 3]
            filled[m][d] = total
            before[m][d] = running
            at_me = at_me + jnp.where(dp == d, running, 0)
            running = running + total
        ls = [lens[m, 4 * dp + c] for c in range(4)]
        ends, starts, run, frun = [], [], jnp.int32(0), jnp.int32(0)
        for c in range(4):
            run = run + ls[c]
            ends.append(run)
            starts.append(frun)
            unit = jnp.where(ls[c] >= 78, 1, 0) + jnp.where(ls[c] >= 156, 1, 0) + jnp.where(ls[c] >= 234, 1, 0) + jnp.where(ls[c] >= 312, 1, 0)
            frun = frun + 784 * unit
        mine.append((at_me, run))
        own.append((ends, starts, frun))

    def picks(d):
        res = []
        for m in range(MICROS):
            lead = (dp - before[m][d]) & (CHIPS - 1)
            first = (before[m][d] + lead) >> 4
            count = (filled[m][d] - lead + CHIPS - 1) >> 4
            res.append((first, count))
        return res

    row48 = _iota((PAIR, RT), 0)
    lane640 = _iota((PAIR, RT), 1)
    second = row48 >= SLOT
    slot48 = jnp.where(second, row48 - SLOT, row48)

    for d in range(CHIPS):
        (fa, na), (fb, nb) = picks(d)
        live = slot48 < jnp.where(second, nb, na)
        want = jnp.where(second, fb + RP, fa) + slot48
        Tb[d * PAIR : (d + 1) * PAIR, :] = jnp.where((lane640 == want) & live, 1.0, 0.0).astype(BF)

    W[f, z, y, x, :, C_DOWN:C_ALL] = wdn[...]
    swap.wait()
    mine_rows = wsw[f, 0:24, :].astype(F32)
    other_rows = swp[0:24, :].astype(F32)
    lower = jnp.where(f == 0, mine_rows, other_rows)
    upper = jnp.where(f == 0, other_rows, mine_rows)
    W[f, z, y, x, :, 0:SWAPPED] = jnp.concatenate([lower, upper], axis=0).astype(BF)
    ag(0, 0)

    tok_load.wait()
    outg[...] = _nn(Tb[...], A[...]).astype(BF).reshape(CHIPS, PAIR, D)
    sends = []
    for k in range(1, CHIPS):
        to = peer(k)
        c = remote(outg.at[to[0]], inc.at[dp], a2, (k - 1,), to)
        c.start()
        sends.append(c)
    inc[dp] = outg[dp]
    ag(1, 0)

    chan = _iota((64, DD), 1)
    even = (chan & 1) == 0
    rate = jnp.exp((chan - (chan & 1)).astype(F32) * (-math.log(10000.0) / DD))
    ang = (32 * _iota((64, DD), 0)).astype(F32) * rate
    sa, ca = jnp.sin(ang), jnp.cos(ang)
    angb = _iota((64, DD), 0).astype(F32) * rate
    sb, cb = jnp.sin(angb), jnp.cos(angb)

    def put(rows, col, val):
        hi = val.astype(BF)
        tab[rows : rows + 64, col : col + DD] = hi
        tab[128 + rows : 128 + rows + 64, col : col + DD] = (val - hi.astype(F32)).astype(BF)

    tab[...] = jnp.zeros_like(tab)
    put(0, 0, jnp.where(even, sa, ca))
    put(0, DD, jnp.where(even, ca, -sa))
    put(64, 2 * DD, cb)
    put(64, 3 * DD, sb)

    lane_p = _iota((1, RP), 1)
    sub_p = _iota((RP, 1), 0)
    diag = _iota((RP, RP), 0) == _iota((RP, RP), 1)
    target_row = []
    target_col = []
    for m in range(MICROS):
        ends, starts, _ = own[m]

        def clip_of(p):
            return sum((jnp.where(p >= e, 1, 0) for e in ends))

        def start_of(cid):
            return sum((jnp.where(cid == c, starts[c], 0) for c in range(4)))

        cr, cc = clip_of(lane_p), clip_of(sub_p)
        bias[m] = jnp.where(cc == cr, 0.0, NEG)
        tr = jnp.where(cr < 4, start_of(cr) + vis[m : m + 1, :], -1)
        vcol = jnp.sum(jnp.where(diag, jnp.broadcast_to(vis[m : m + 1, :].astype(F32), (RP, RP)), 0.0), axis=1, keepdims=True)
        tc = jnp.where(cc < 4, start_of(cc) + vcol.astype(jnp.int32), -1)
        target_row.append(tr)
        target_col.append(tc)

    def project_back(m):
        y_load[m].wait()
        full_total = own[m][2]
        extra = sub_p == RP - 1

        def chunk(c, acc):
            spot = _iota((RP, YC), 1) + c * YC
            hit = (spot == target_col[m]) | (extra & (spot < full_total))
            ys = big[pl.ds(pl.multiple_of(m * FULL + c * YC, 64), YC), :]
            return acc + _nn(jnp.where(hit, 1.0, 0.0).astype(BF), ys)

        acc = lax.fori_loop(0, FULL // YC, chunk, jnp.zeros((RP, DD), F32))
        whole = jnp.sum(jnp.where(extra, acc, 0.0), axis=0, keepdims=True)
        acc = jnp.where(extra, 0.0, acc)
        dZ[m * RP : (m + 1) * RP, :] = acc.astype(BF)
        return whole - jnp.sum(acc, axis=0, keepdims=True)

    ag(0, 1)
    mask_sum = project_back(0)
    ag(0, 2)
    mask_sum = mask_sum + project_back(1)
    ag(0, 3)
    ag(1, 1)
    ag(2, 0)

    for c in sends:
        c.wait()
    for m in range(MICROS):
        off, count = mine[m]
        want = ((off + sub_p) & (CHIPS - 1)) * PAIR + m * SLOT + (sub_p >> 4)
        want = jnp.where(sub_p < count, want, -1)
        hit = jnp.where(_iota((RP, CHIPS * PAIR), 1) == want, 1.0, 0.0).astype(BF)
        X[m * RP : (m + 1) * RP, :] = _nn(hit, inc[...].reshape(CHIPS * PAIR, D)).astype(BF)

    ag(0, 4)

    def wt(h, c0, n):
        return W[h, :, :, :, :, c0 : c0 + n].reshape(D, n)

    gains = jnp.transpose(wt(1, C_DEC + 128, 128).astype(F32))
    gain_attn = gains[0:1, :]
    gain_mlp = gains[1:2, :]

    def ln_parts(v):
        center = v - jnp.mean(v, axis=-1, keepdims=True)
        r = lax.rsqrt(jnp.mean(center * center, axis=-1, keepdims=True) + EPS)
        return center * r, r

    def rows(m):
        return pl.ds(m * RP, RP)

    for m in range(MICROS):
        xhat, _ = ln_parts(X[rows(m), :].astype(F32))
        A[rows(m), :] = (xhat * gain_attn).astype(BF)
    for m in range(MICROS):
        for h in range(2):
            Q[rows(m), h * 1152 : (h + 1) * 1152] = _nn(A[rows(m), :], wt(h, C_QKV, 1152)).astype(BF)

    lane128 = _iota((1, 128), 1)
    head_mask = (lane128 < 64, lane128 >= 64)
    QB = ((0, 128), (128, 128), (256, 64))

    def attend(m):
        r0 = m * RP

        def pair(j, carry):
            col = pl.multiple_of(j * 128, 128)
            q2 = Q[r0 : r0 + RP, pl.ds(col, 128)]
            k2 = Q[r0 : r0 + RP, pl.ds(pl.multiple_of(col + D, 128), 128)]
            v_t = jnp.transpose(Q[r0 : r0 + RP, pl.ds(pl.multiple_of(col + 2 * D, 128), 128)])
            for b0, bn in QB:
                halves = []
                for h in range(2):
                    qm = jnp.where(head_mask[h], q2[b0 : b0 + bn], jnp.zeros((), BF))
                    s = _nt(k2, qm) * 0.125 + bias[m, :, b0 : b0 + bn]
                    e = jnp.exp(s - jnp.max(s, axis=0, keepdims=True))
                    p = (e * (1.0 / jnp.sum(e, axis=0, keepdims=True))).astype(BF)
                    at = pl.multiple_of((m * 12 + 2 * j + h) * RP, 64)
                    big[pl.ds(at, RP), b0 : b0 + bn] = p
                    halves.append(_nn(v_t[64 * h : 64 * h + 64], p))
                O[r0 + b0 : r0 + b0 + bn, pl.ds(col, 128)] = jnp.transpose(jnp.concatenate(halves, axis=0)).astype(BF)
            return carry

        lax.fori_loop(0, 6, pair, 0)

    ag(1, 2)
    attend(0)
    ag(1, 3)
    ag(2, 1)
    attend(1)
    ag(1, 4)
    ag(2, 2)

    w_out = jnp.concatenate([wt(0, C_OUT, 384), wt(1, C_OUT, 384)], axis=1)
    for m in range(MICROS):
        x1 = X[rows(m), :].astype(F32) + _nn(O[rows(m), :], w_out)
        X1[rows(m), :] = x1
        xhat, _ = ln_parts(x1)
        H[rows(m), :] = (xhat * gain_mlp).astype(BF)

    for h in range(2):
        for blk in range(2):
            w = wt(h, C_UP + blk * 768, 768)
            c0 = (2 * h + blk) * 768

            def up(m, carry, w=w, c0=c0):
                at = pl.ds(pl.multiple_of(m * RP, RP), RP)
                u = _nn(H[at, :], w)
                cdf = 0.5 * (1.0 + lax.erf(u * (1.0 / math.sqrt(2.0))))
                pdf = jnp.exp(u * u * -0.5) * (1.0 / math.sqrt(2.0 * math.pi))
                G[at, c0 : c0 + 768] = (u * cdf).astype(BF)
                GP[at, c0 : c0 + 768] = (cdf + u * pdf).astype(BF)
                return carry

            lax.fori_loop(0, MICROS, up, 0)
        if h == 0:
            ag(2, 3)

    w_dec = jnp.concatenate([wt(0, C_DEC, 256), wt(1, C_DEC, 128)], axis=1)
    for m in range(MICROS):
        d = _nt(dZ[rows(m), :], w_dec)
        dX[rows(m), :] = d
        dW[rows(m), :] = d.astype(BF)

    def put_grad(ref, h, c0, n, val):
        ref[h, :, :, :, :, c0 : c0 + n] = val.astype(BF).reshape(NZ, NY, NX, CH, n)

    for h in range(2):
        for blk in range(2):
            c0 = (2 * h + blk) * 768
            put_grad(gD, h, blk * 768, 768, _tn(G[:, c0 : c0 + 768], dW[...]))
    rs_a(DOWN)
    ag(2, 4)

    for m in range(MICROS):
        acc = X1[rows(m), :]
        for h in range(2):
            for blk in range(2):
                c0 = (2 * h + blk) * 768
                acc = acc + _nn(G[rows(m), c0 : c0 + 768], wt(h, C_DOWN + blk * 768, 768))
        X2[rows(m), :] = acc.astype(BF)
    for m in range(MICROS):
        Zx[rows(m), 0:DD] = _nn(X2[rows(m), :], w_dec).astype(BF)
        Zx[rows(m), DD:512] = jnp.ones((RP, 128), BF)
    gd = _tn(X2[...], dZ[...])
    put_grad(W, 0, C_DEC, 256, gd[:, 0:256])
    put_grad(W, 1, C_DEC, 128, gd[:, 256:384])
    rs_a(DEC)
    rs_b(DOWN)

    for h in range(2):
        for blk in range(2):
            c0 = (2 * h + blk) * 768
            for m in range(MICROS):
                back = _nt(dW[rows(m), :], wt(h, C_DOWN + blk * 768, 768))
                GP[rows(m), c0 : c0 + 768] = (back * GP[rows(m), c0 : c0 + 768].astype(F32)).astype(BF)
    rs_c(DOWN)
    rs_b(DEC)

    Tb[...] = jnp.transpose(H[...])
    for h in range(2):
        for blk in range(2):
            c0 = (2 * h + blk) * 768
            put_grad(W, h, C_DOWN + blk * 768, 768, _nn(Tb[...], GP[:, c0 : c0 + 768]))
    rs_a(UP)
    rs_d(DOWN)
    rs_c(DEC)

    gain_sums = [None, None]
    for m in range(MICROS):
        dh = _nt(GP[rows(m), 0:1536], wt(0, C_UP, 1536)) + _nt(GP[rows(m), 1536:3072], wt(1, C_UP, 1536))
        xhat, r = ln_parts(X1[rows(m), :])
        gsum = jnp.sum(dh * xhat, axis=0, keepdims=True)
        gain_sums[1] = gsum if m == 0 else gain_sums[1] + gsum
        dxh = dh * gain_mlp
        back = r * (dxh - jnp.mean(dxh, axis=-1, keepdims=True) - xhat * jnp.mean(dxh * xhat, axis=-1, keepdims=True))
        dx1 = dX[rows(m), :] + back
        dX[rows(m), :] = dx1
        dW[rows(m), :] = dx1.astype(BF)
    rs_b(UP)
    rs_e(DOWN)
    rs_d(DEC)

    w_out = jnp.concatenate([wt(0, C_OUT, 384), wt(1, C_OUT, 384)], axis=1)
    dO = X2
    for m in range(MICROS):
        dO[rows(m), :] = _nt(dW[rows(m), :], w_out).astype(BF)
    go = _tn(O[...], dW[...])
    put_grad(W, 0, C_OUT, 384, go[:, 0:384])
    put_grad(W, 1, C_OUT, 384, go[:, 384:768])
    rs_a(OUT)
    rs_c(UP)
    rs_e(DEC)
    rs_b(OUT)

    def attend_back(m):
        r0 = m * RP

        def pair(j, carry):
            col = pl.multiple_of(j * 128, 128)
            cq, ck, cv = pl.ds(col, 128), pl.ds(pl.multiple_of(col + D, 128), 128), pl.ds(pl.multiple_of(col + 2 * D, 128), 128)
            q2, k2, v2 = Q[r0 : r0 + RP, cq], Q[r0 : r0 + RP, ck], Q[r0 : r0 + RP, cv]
            do2 = dO[r0 : r0 + RP, cq]
            k_t = jnp.transpose(k2)
            dk = jnp.zeros((RP, 128), F32)
            dv = jnp.zeros((RP, 128), F32)
            for b0, bn in QB:
                halves = []
                for h in range(2):
                    dom = jnp.where(head_mask[h], do2[b0 : b0 + bn], jnp.zeros((), BF))
                    qm = jnp.where(head_mask[h], q2[b0 : b0 + bn], jnp.zeros((), BF))
                    dp_t = _nt(v2, dom)
                    at = pl.multiple_of((m * 12 + 2 * j + h) * RP, 64)
                    pb = big[pl.ds(at, RP), b0 : b0 + bn]
                    p = pb.astype(F32)
                    w = p * dp_t
                    ds = (w - p * jnp.sum(w, axis=0, keepdims=True)).astype(BF)
                    halves.append(_nn(k_t[64 * h : 64 * h + 64], ds))
                    dv = dv + _nn(pb, dom)
                    dk = dk + _nn(ds, qm)
                dq = jnp.transpose(jnp.concatenate(halves, axis=0)) * 0.125
                Q[r0 + b0 : r0 + b0 + bn, cq] = dq.astype(BF)
            Q[r0 : r0 + RP, ck] = (dk * 0.125).astype(BF)
            Q[r0 : r0 + RP, cv] = dv.astype(BF)
            return carry

        lax.fori_loop(0, 6, pair, 0)

    attend_back(0)
    rs_d(UP)
    rs_c(OUT)
    rs_f(DEC)
    attend_back(1)
    rs_e(UP)
    rs_d(OUT)

    for m in range(MICROS):
        da = _nt(Q[rows(m), 0:1152], wt(0, C_QKV, 1152)) + _nt(Q[rows(m), 1152:2304], wt(1, C_QKV, 1152))
        xhat, r = ln_parts(X[rows(m), :].astype(F32))
        gsum = jnp.sum(da * xhat, axis=0, keepdims=True)
        gain_sums[0] = gsum if m == 0 else gain_sums[0] + gsum
        dxh = da * gain_attn
        back = r * (dxh - jnp.mean(dxh, axis=-1, keepdims=True) - xhat * jnp.mean(dxh * xhat, axis=-1, keepdims=True))
        H[rows(m), :] = (dX[rows(m), :] + back).astype(BF)

    vec[...] = jnp.concatenate(
        [mask_sum, gain_sums[0][:, 0:384], gain_sums[0][:, 384:768], gain_sums[1][:, 0:384], gain_sums[1][:, 384:768], jnp.zeros((3, DD), F32)],
        axis=0,
    )
    vec_flight = []

    def vec_send(to, i):
        c = remote(vec, rv.at[i], rvk, (i,), to)
        c.start()
        return c

    vc = vec_send(sib, 0)

    for d in range(CHIPS):
        lead = [(d - mine[m][0]) & (CHIPS - 1) for m in range(MICROS)]
        want = jnp.where(second, lead[1], lead[0]) + slot48 * CHIPS
        live = want < jnp.where(second, mine[1][1], mine[0][1])
        want = want + jnp.where(second, RP, 0)
        Tb[d * PAIR : (d + 1) * PAIR, :] = jnp.where((lane640 == want) & live, 1.0, 0.0).astype(BF)
    outg[...] = _nn(Tb[...], H[...]).astype(BF).reshape(CHIPS, PAIR, D)
    sends = []
    for k in range(1, CHIPS):
        to = peer(k)
        c = remote(outg.at[to[0]], incb.at[dp], a2b, (k - 1,), to)
        c.start()
        sends.append(c)
    incb[dp] = outg[dp]

    Tb[...] = jnp.transpose(A[...])
    for h in range(2):
        put_grad(W, h, C_UP, 1152, _nn(Tb[...], Q[:, h * 1152 : (h + 1) * 1152]))
    rs_a(QKV)
    rs_e(OUT)
    rs_f(UP)

    def decode(m, lo, hi):
        full_total = own[m][2]
        mt = mask_tok[...].astype(F32)

        def chunk(c, carry):
            spot = _iota((EC, RP), 0) + c * EC
            hit = jnp.where(spot == target_row[m], 1.0, 0.0).astype(BF)
            mz = _nn(hit, Zx[rows(m), :])
            ps = pos[m, pl.ds(c, 1), :]
            kk = _iota((256, EC), 0) & 127
            want = jnp.where(kk < 64, ps >> 5, (ps & 31) + 64)
            code = _tn(jnp.where(kk == want, 1.0, 0.0).astype(BF), tab[...])
            pe = code[:, 0:DD] * code[:, 2 * DD : 3 * DD] + code[:, DD : 2 * DD] * code[:, 3 * DD : 4 * DD]
            live = jnp.where(_iota((EC, 1), 0) + c * EC < full_total, 1.0, 0.0)
            cov = jnp.concatenate([mz[:, DD:512]] * 3, axis=1)
            val = mz[:, 0:DD] + (live - cov) * mt + live * pe
            big[pl.ds(pl.multiple_of(m * FULL + c * EC, 32), EC), :] = val.astype(BF)
            return carry

        lax.fori_loop(lo, hi, chunk, 0)

    decode(0, 0, 7)
    rs_b(QKV)
    vc.wait()
    vec[...] = vec[...] + rv[0]
    vc = vec_send(xn, 1)
    rs_f(OUT)
    decode(0, 7, 14)
    dec_out = [pltpu.make_async_copy(big.at[pl.ds(0, FULL)], o_dec.at[0], ok.at[0])]
    dec_out[0].start()
    rs_c(QKV)
    vc.wait()
    vec[...] = vec[...] + rv[1]
    vc = vec_send(yn, 2)
    decode(1, 0, 7)
    rs_d(QKV)
    vc.wait()
    vec[...] = vec[...] + rv[2]
    vcs = []
    for k in range(1, NZ):
        vcs.append(remote(vec, rv.at[2 + k], rvk, (2 + k,), dev_z(k)))
        vcs[-1].start()
    decode(1, 7, 14)
    dec_out.append(pltpu.make_async_copy(big.at[pl.ds(FULL, FULL)], o_dec.at[1], ok.at[1]))
    dec_out[1].start()
    rs_e(QKV)

    lane768 = _iota((1, CHIPS * PAIR), 1)
    want = jnp.full((1, CHIPS * PAIR), -1, jnp.int32)
    for d in range(CHIPS):
        (fa, na), (fb, nb) = picks(d)
        s = lane768 - d * PAIR
        want = jnp.where((s >= 0) & (s < na), fa + s, want)
        s = s - SLOT
        want = jnp.where((s >= 0) & (s < nb), RP + fb + s, want)
    for c in sends:
        c.wait()
    for m in range(MICROS):
        hit = jnp.where(_iota((RP, CHIPS * PAIR), 0) + m * RP == want, 1.0, 0.0).astype(BF)
        back = _nn(hit, incb[...].reshape(CHIPS * PAIR, D)).astype(BF)
        o_tok[m] = back[0 : o_tok.shape[1]]
    for c in vcs:
        c.wait()
    o_vec[...] = vec[...] + rv[3] + rv[4] + rv[5]
    rs_f(QKV)
    for c in dec_out:
        c.wait()


def _mega_call(tok, wsw, wdn, mask_tok, lens, vis, pos, cot):
    rows_in = cot.shape[1]
    vm = lambda *s: pltpu.VMEM(s[:-1], s[-1])
    sem = lambda *s: pltpu.SemaphoreType.DMA(s)
    V = pl.BlockSpec(memory_space=pltpu.VMEM)
    S = pl.BlockSpec(memory_space=pltpu.SMEM)
    ANY = pl.BlockSpec(memory_space=pl.ANY)
    scratch = [
        vm(2, NZ, NY, NX, CH, C_ALL, BF),
        vm(2, NZ, NY, NX, CH, 1536, BF),
        vm(24 * RP, DD, BF),
        vm(RT, D, BF),
        vm(RT, D, BF),
        vm(D, RT, BF),
        vm(RT, 3 * D, BF),
        vm(RT, D, BF),
        vm(RT, D, F32),
        vm(RT, D, BF),
        vm(RT, 4 * D, BF),
        vm(RT, 4 * D, BF),
        vm(RT, D, BF),
        vm(RT, DD, BF),
        vm(RT, D, F32),
        vm(RT, D, BF),
        vm(RT, 512, BF),
        vm(CHIPS, PAIR, D, BF),
        vm(CHIPS, PAIR, D, BF),
        vm(CHIPS, PAIR, D, BF),
        vm(MICROS, RP, RP, F32),
        vm(256, 4 * DD, BF),
        vm(32, SWAPPED, BF),
        vm(2, 2, 2, CH, 1536, BF),
        vm(3, CH, C_ALL, BF),
        vm(24, SWAPPED, F32),
        vm(CH, SWAPPED, F32),
        vm(8, DD, F32),
        vm(6, 8, DD, F32),
    ]
    hbm = lambda *s: jax.ShapeDtypeStruct(s, BF)
    sems = [
        sem(2), sem(2, 1), sem(2, 3, 3), sem(2, 3, 2), sem(2, 3, 2), sem(2, 3), sem(2, 15), sem(2, 15),
        sem(2, 5), sem(2, 5, 2), sem(2, 5, 2), sem(2, 5, 3), sem(2, 5), sem(2, 6), sem(2), sem(2), sem(1),
    ]
    n_out = 5
    n_hbm = 5

    def kern(*refs):
        ins, rest = refs[:8], refs[8:]
        outs, hb, rest = rest[:n_out], rest[n_out : n_out + n_hbm], rest[n_out + n_hbm :]
        scr, sm = rest[: len(scratch)], rest[len(scratch) :]
        _mega(*ins, *outs, *scr, *hb, *sm)

    out = pl.pallas_call(
        kern,
        out_shape=[
            jax.ShapeDtypeStruct((MICROS, FULL, DD), BF),
            jax.ShapeDtypeStruct((MICROS, 314, D), BF),
            jax.ShapeDtypeStruct((2, 24, SWAPPED), F32),
            jax.ShapeDtypeStruct((CH, 1536), F32),
            jax.ShapeDtypeStruct((8, DD), F32),
            hbm(NZ, NY, NX, CH, C_ALL),
            hbm(NZ, 2, CH, 2432),
            hbm(NZ, 2, CH, 2432),
            hbm(NZ, CH, 2432),
            hbm(NZ, CH, 2432),
        ],
        in_specs=[ANY, V, V, V, S, V, V, ANY],
        out_specs=[ANY, V, V, V, V] + [ANY] * n_hbm,
        scratch_shapes=scratch + sems,
        compiler_params=pltpu.CompilerParams(collective_id=0, has_side_effects=True, vmem_limit_bytes=63 * 2**20),
    )(tok, wsw, wdn, mask_tok, lens, vis, pos, cot)
    return out[:n_out]


def _halves(w):
    n = w.shape[1] // 2
    return w[:, :n], w[:, n:]


def _deal(w):
    r = w.shape[0]
    return w.reshape(r, CHIPS, 2, 2, CH).transpose(0, 2, 3, 1, 4).reshape(r, 4 * D)


def _undeal(w):
    r = w.shape[0]
    return w.reshape(r, 2, 2, CHIPS, CH).transpose(0, 3, 1, 2, 4).reshape(r, 4 * D)


def per_device_fused(
    tokens, gain_attn, gain_mlp, w_qkv, w_out, w_up, w_down, w_dec, mask_token, clip_lengths, vis_index, pos_index, cotangent,
):
    row_count = tokens.shape[2]
    tok = jnp.pad(tokens[0], ((0, 0), (0, RP - row_count), (0, 0))).reshape(RT, D)
    dec = jnp.concatenate([w_dec, gain_attn[:, None], gain_mlp[:, None], jnp.zeros((w_dec.shape[0], 126), BF)], axis=1)
    parts = [_halves(w_qkv), _halves(dec), _halves(w_out), _halves(_deal(w_up))]
    wsw = jnp.stack([jnp.concatenate([p[h] for p in parts], axis=1) for h in range(2)])
    wsw = jnp.pad(wsw, ((0, 0), (0, 8), (0, 0)))
    wdn = jnp.concatenate([w_down[:CH], w_down[CH:]], axis=1)
    vis = jnp.pad(vis_index[0], ((0, 0), (0, RP - row_count)))
    pos = pos_index[0].reshape(MICROS, FULL // EC, EC)
    decoded, returned, cat, dn, vec = _mega_call(tok, wsw, wdn, mask_token[None], clip_lengths[0], vis, pos, cotangent[0])

    def panel(c0, n):
        return jnp.concatenate([cat[0, :, c0 : c0 + n], cat[1, :, c0 : c0 + n]], axis=1)

    me = lax.axis_index("dp") * 2 + lax.axis_index("fsdp")
    ga = lax.dynamic_slice(vec[1:3].reshape(-1), (24 * me,), (24,))
    gm = lax.dynamic_slice(vec[3:5].reshape(-1), (24 * me,), (24,))
    return (
        decoded[None],
        returned[None],
        ga,
        gm,
        panel(C_QKV, 1152),
        panel(C_OUT, 384),
        _undeal(panel(C_UP, 1536)),
        jnp.concatenate([dn[:, :D], dn[:, D:]], axis=0),
        panel(C_DEC, 256)[:, :DD],
        vec[0],
    )


def solution(mesh):
    in_specs = (
        P("fsdp", None, "dp", None),
        P(("dp", "fsdp")),
        P(("dp", "fsdp")),
        P(("dp", "fsdp"), None),
        P(("dp", "fsdp"), None),
        P(("dp", "fsdp"), None),
        P(("dp", "fsdp"), None),
        P(("dp", "fsdp"), None),
        P(),
        P("fsdp", None, None),
        P("fsdp", None, "dp"),
        P("fsdp", None, "dp"),
        P("fsdp", None, "dp", None),
    )
    out_specs = (
        P("fsdp", None, "dp", None),
        P("fsdp", None, "dp", None),
        P(("dp", "fsdp")),
        P(("dp", "fsdp")),
        P(("dp", "fsdp"), None),
        P(("dp", "fsdp"), None),
        P(("dp", "fsdp"), None),
        P(("dp", "fsdp"), None),
        P(("dp", "fsdp"), None),
        P(),
    )
    body = per_device_fused if mesh.shape["dp"] == CHIPS and mesh.shape["fsdp"] == 2 else per_device
    return jax.shard_map(
        body, mesh=mesh, in_specs=in_specs, out_specs=out_specs, check_vma=False
    )
```

```python
import math

import jax
import jax.numpy as jnp
from jax import lax
from jax.experimental import pallas as pl
from jax.experimental.pallas import tpu as pltpu
from jax.sharding import PartitionSpec as P

HEADS = 12
HEAD = 64
SHORT = 78
FULL_UNIT = 784


NEG = -1e30
EPS = 1e-06


def layer_norm(values, scale_gain):
    center = values - jnp.mean(values, axis=-1, keepdims=True)
    spread = jnp.mean(center * center, axis=-1, keepdims=True)
    return center * lax.rsqrt(spread + EPS) * scale_gain


def softmax_rows(scores):
    shifted = scores - jnp.max(scores, axis=-1, keepdims=True)
    powers = jnp.exp(shifted)
    return powers / jnp.sum(powers, axis=-1, keepdims=True)


def gelu_exact(values):
    return 0.5 * values * (1.0 + lax.erf(values * (1.0 / math.sqrt(2.0))))


def sinusoid(table_index, features):
    channel = jnp.arange(features)
    rates = jnp.exp((channel // 2 * 2).astype(jnp.float32) * (-math.log(10000.0) / features))
    angles = table_index.astype(jnp.float32)[:, None] * rates[None, :]
    return jnp.where(channel % 2 == 0, jnp.sin(angles), jnp.cos(angles))


def block_layout(lengths, row_count):
    clip_ends = jnp.cumsum(lengths)
    full_sizes = lengths // SHORT * FULL_UNIT
    full_ends = jnp.cumsum(full_sizes)
    full_starts = full_ends - full_sizes
    row_ids = jnp.arange(row_count)
    clip_of = jnp.sum((row_ids[:, None] >= clip_ends[None, :]).astype(jnp.int32), axis=1)
    live_rows = clip_of < lengths.shape[0]
    slot_ids = jnp.arange(lengths.shape[0])
    start_of = jnp.sum(
        jnp.where(clip_of[:, None] == slot_ids[None, :], full_starts[None, :], 0), axis=1
    )
    return (clip_of, live_rows, start_of, full_ends[-1])


def contract(left_side, right_side, pattern):
    return jnp.einsum(pattern, left_side, right_side, preferred_element_type=jnp.float32)


def layer_pass(block_in, lengths, visible, position, grad_rows, params, mask_token):
    gain_attn, gain_mlp, w_qkv, w_out, w_up, w_down, w_dec = params
    row_count = block_in.shape[0]
    features = block_in.shape[1]
    full_count = grad_rows.shape[0]
    clip_of, live_rows, start_of, total_full = block_layout(lengths, row_count)
    same_clip = clip_of[:, None] == clip_of[None, :]
    inputs = block_in.astype(jnp.float32)
    normed, norm_attn_back = jax.vjp(layer_norm, inputs, gain_attn.astype(jnp.float32))
    normed = normed.astype(jnp.bfloat16)
    mixed_qkv = contract(normed, w_qkv, "pc,ce->pe").astype(jnp.bfloat16)
    queries = mixed_qkv[:, :features].reshape(row_count, HEADS, HEAD)
    key_rows = mixed_qkv[:, features : 2 * features].reshape(row_count, HEADS, HEAD)
    value_rows = mixed_qkv[:, 2 * features :].reshape(row_count, HEADS, HEAD)
    scores = contract(queries, key_rows, "qhd,khd->hqk") * HEAD ** (-0.5)
    scores = jnp.where(same_clip[None], scores, NEG)
    weights, soft_back = jax.vjp(softmax_rows, scores)
    weights_low = weights.astype(jnp.bfloat16)
    attended = (
        contract(weights_low, value_rows, "hqk,khd->qhd")
        .reshape(row_count, features)
        .astype(jnp.bfloat16)
    )
    after_attn = inputs + contract(attended, w_out, "pc,ce->pe")
    hidden, norm_mlp_back = jax.vjp(layer_norm, after_attn, gain_mlp.astype(jnp.float32))
    hidden = hidden.astype(jnp.bfloat16)
    upward = contract(hidden, w_up, "pc,cf->pf")
    activated, gelu_back = jax.vjp(gelu_exact, upward)
    activated = activated.astype(jnp.bfloat16)
    after_mlp = after_attn + contract(activated, w_down, "pf,fc->pc")
    final_low = after_mlp.astype(jnp.bfloat16)
    projected = contract(final_low, w_dec, "pc,ce->pe").astype(jnp.bfloat16)
    full_index = jnp.arange(full_count)
    target = start_of + visible
    place_map = ((full_index[:, None] == target[None, :]) & live_rows[None, :]).astype(jnp.bfloat16)
    covered = jnp.sum(place_map, axis=1, dtype=jnp.float32)
    full_live = (full_index < total_full).astype(jnp.float32)
    masked_share = full_live - covered
    decoded = (
        contract(place_map, projected, "ip,pe->ie")
        + masked_share[:, None] * mask_token.astype(jnp.float32)[None, :]
        + full_live[:, None] * sinusoid(position, projected.shape[1])
    )
    grad_full = grad_rows.astype(jnp.float32)
    mask_term = jnp.sum(masked_share[:, None] * grad_full, axis=0)
    back_proj = contract(place_map, grad_rows, "ip,ie->pe").astype(jnp.bfloat16)
    grad_dec = contract(final_low, back_proj, "pc,pe->ce")
    back_final = contract(back_proj, w_dec, "pe,ce->pc")
    back_mlp = back_final.astype(jnp.bfloat16)
    grad_down = contract(activated, back_mlp, "pf,pc->fc")
    back_act = contract(back_mlp, w_down, "pc,fc->pf")
    back_up = gelu_back(back_act)[0].astype(jnp.bfloat16)
    grad_up = contract(hidden, back_up, "pc,pf->cf")
    back_hidden = contract(back_up, w_up, "pf,cf->pc")
    back_norm_mlp, grad_gain_mlp = norm_mlp_back(back_hidden)
    back_after = back_final + back_norm_mlp
    back_attn_out = back_after.astype(jnp.bfloat16)
    grad_out = contract(attended, back_attn_out, "pc,pe->ce")
    back_attended = (
        contract(back_attn_out, w_out, "pe,ce->pc")
        .astype(jnp.bfloat16)
        .reshape(row_count, HEADS, HEAD)
    )
    back_weights = contract(back_attended, value_rows, "qhd,khd->hqk")
    back_values = contract(weights_low, back_attended, "hqk,qhd->khd")
    back_scores = soft_back(back_weights)[0].astype(jnp.bfloat16) * HEAD ** (-0.5)
    back_queries = contract(back_scores, key_rows, "hqk,khd->qhd")
    back_keys = contract(back_scores, queries, "hqk,qhd->khd")
    back_mixed = jnp.concatenate(
        [
            back_queries.reshape(row_count, features),
            back_keys.reshape(row_count, features),
            back_values.reshape(row_count, features),
        ],
        axis=1,
    ).astype(jnp.bfloat16)
    grad_qkv = contract(normed, back_mixed, "pc,pe->ce")
    back_normed = contract(back_mixed, w_qkv, "pe,ce->pc")
    back_inputs, grad_gain_attn = norm_attn_back(back_normed)
    back_block = (back_after + back_inputs).astype(jnp.bfloat16)
    gradients = (grad_gain_attn, grad_gain_mlp, grad_qkv, grad_out, grad_up, grad_down, grad_dec)
    return (decoded.astype(jnp.bfloat16), back_block, gradients, mask_term)


def per_device(
    tokens,
    gain_attn,
    gain_mlp,
    w_qkv,
    w_out,
    w_up,
    w_down,
    w_dec,
    mask_token,
    clip_lengths,
    vis_index,
    pos_index,
    cotangent,
):
    shards = (gain_attn, gain_mlp, w_qkv, w_out, w_up, w_down, w_dec)
    spread = lax.axis_size(("dp", "fsdp"))
    running = tuple(
        (jnp.zeros((piece.shape[0] * spread,) + piece.shape[1:], jnp.float32) for piece in shards)
    )
    devices = lax.axis_size("dp")
    device = lax.axis_index("dp")
    micro_count = tokens.shape[1]
    row_count = tokens.shape[2]
    features = tokens.shape[3]
    slot_count = -(-row_count // devices)
    mask_sum = jnp.zeros(mask_token.shape, jnp.float32)
    decoded_all = []
    returned_all = []
    for micro_step in range(micro_count):
        params = (
            lax.all_gather(shards[0], ("dp", "fsdp"), axis=0, tiled=True),
            lax.all_gather(shards[1], ("dp", "fsdp"), axis=0, tiled=True),
            lax.all_gather(shards[2], ("dp", "fsdp"), axis=0, tiled=True),
            lax.all_gather(shards[3], ("dp", "fsdp"), axis=0, tiled=True),
            lax.all_gather(shards[4], ("dp", "fsdp"), axis=0, tiled=True),
            lax.all_gather(shards[5], ("dp", "fsdp"), axis=0, tiled=True),
            lax.all_gather(shards[6], ("dp", "fsdp"), axis=0, tiled=True),
        )
        lengths = clip_lengths[0, micro_step].reshape(devices, -1)
        filled = jnp.sum(lengths, axis=1)
        offsets = jnp.cumsum(filled) - filled
        leading = (device - offsets) % devices
        first_row = (offsets + leading) // devices
        slot_index = jnp.arange(slot_count)
        sent_live = leading[None, :] + slot_index[:, None] * devices < filled[None, :]
        pick_rows = jnp.where(sent_live, first_row[None, :] + slot_index[:, None], row_count)
        source_rows = jnp.concatenate(
            [tokens[0, micro_step], jnp.zeros((1, features), tokens.dtype)], axis=0
        )
        outgoing = jnp.take(source_rows, pick_rows, axis=0)
        incoming = lax.all_to_all(outgoing, "dp", split_axis=1, concat_axis=1, tiled=True)
        own_offset = lax.dynamic_index_in_dim(offsets, device, 0, keepdims=False)
        block_in = jnp.roll(incoming, -own_offset, axis=1).reshape(slot_count * devices, features)[
            :row_count
        ]
        own_lengths = lax.dynamic_index_in_dim(lengths, device, 0, keepdims=False)
        decoded, back_block, gradients, mask_term = layer_pass(
            block_in,
            own_lengths,
            vis_index[0, micro_step],
            pos_index[0, micro_step],
            cotangent[0, micro_step],
            params,
            mask_token,
        )
        running = tuple(
            (total_piece + new_piece for total_piece, new_piece in zip(running, gradients))
        )
        mask_sum = mask_sum + mask_term
        padded_back = jnp.concatenate(
            [back_block, jnp.zeros((slot_count * devices - row_count, features), jnp.bfloat16)],
            axis=0,
        )
        outgoing_back = jnp.roll(
            padded_back.reshape(slot_count, devices, features), own_offset, axis=1
        )
        incoming_back = lax.all_to_all(outgoing_back, "dp", split_axis=1, concat_axis=1, tiled=True)
        returned = (
            jnp.zeros((row_count + 1, features), jnp.bfloat16)
            .at[pick_rows]
            .add(incoming_back)[:row_count]
        )
        decoded_all.append(decoded)
        returned_all.append(returned)
    shares = (
        lax.psum_scatter(running[0], ("dp", "fsdp"), scatter_dimension=0, tiled=True),
        lax.psum_scatter(running[1], ("dp", "fsdp"), scatter_dimension=0, tiled=True),
        lax.psum_scatter(running[2], ("dp", "fsdp"), scatter_dimension=0, tiled=True),
        lax.psum_scatter(running[3], ("dp", "fsdp"), scatter_dimension=0, tiled=True),
        lax.psum_scatter(running[4], ("dp", "fsdp"), scatter_dimension=0, tiled=True),
        lax.psum_scatter(running[5], ("dp", "fsdp"), scatter_dimension=0, tiled=True),
        lax.psum_scatter(running[6], ("dp", "fsdp"), scatter_dimension=0, tiled=True),
    )
    mask_grad = lax.psum(mask_sum, ("dp", "fsdp"))
    return (
        jnp.stack(decoded_all)[None],
        jnp.stack(returned_all)[None],
        shares[0],
        shares[1],
        shares[2],
        shares[3],
        shares[4],
        shares[5],
        shares[6],
        mask_grad,
    )


BF = jnp.bfloat16
F32 = jnp.float32
MESH = pl.DeviceIdType.MESH
MICROS = 2
RP = 320
RT = MICROS * RP
D = 768
DD = 384
FULL = 3136
NZ, NY, NX = 4, 2, 2
CHIPS = NZ * NY * NX
CH = 48
PK = 1024
C_QKV = (0, 640, 1024)
C_DEC, C_OUT, C_UP, C_DOWN, C_ALL = 384, 1408, 1792, 3328, 4864
SWAPPED = C_DOWN
GATHERS = (
    (0, 384, 640),
    (640, 128, 384),
    (1024, 256, 384),
    (C_OUT, 128, 384),
    (C_UP, 384, 768),
    (C_UP + 768, 384, 768),
    (C_DOWN, 384, 768),
    (C_DOWN + 768, 384, 768),
)
SUMS = (
    (True, 0, 384, 768),
    (True, 768, 384, 768),
    (False, C_DEC, 128, 256),
    (False, C_DOWN, 384, 768),
    (False, C_DOWN + 768, 384, 768),
    (False, C_OUT, 128, 384),
    (False, C_UP, 256, 384),
    (False, C_UP + 384, 128, 384),
    (False, C_UP + 768, 256, 384),
)
SUM_AT = (0, 768, 1536, 1792, 2560, 3328, 3712, 4096, 4480)
SLOTS = 3
YC = 448
EC = 224


(
    S_BEGIN, S_COMPOSE, S_LOAD, S_SEND, S_LAYOUT, S_PROJ, S_BLOCKS, S_GAINS, S_LN1, S_QKV, S_ATT, S_X1, S_UP, S_BDEC,
    S_GDOWN, S_X2, S_Z, S_BDOWN, S_GUP, S_BUP, S_BOUT, S_ATTB, S_BQKV, S_RET, S_GQKV, S_TAB, S_DEC, S_COLL, S_VEC, S_END,
    S_G, S_R,
) = range(32)


def _nn(a, b):
    return lax.dot_general(a, b, (((1,), (0,)), ((), ())), preferred_element_type=F32)


def _nt(a, b):
    return lax.dot_general(a, b, (((1,), (1,)), ((), ())), preferred_element_type=F32)


def _tn(a, b):
    return lax.dot_general(a, b, (((0,), (0,)), ((), ())), preferred_element_type=F32)


def _iota(shape, dim):
    return lax.broadcasted_iota(jnp.int32, shape, dim)


def _mega(
    tok, i0, i1, i2, i3, i4, i5, i6, i7, i8, i9, i10, cot,
    o_rows, o_tok, e0, e1, e2, e3, e4, e5,
    w_qkv, w_out, w_up, w_dec, w_down, gain_a, gain_m, mask_tok, lens, vis, pos,
    o_qkv, o_out, o_up, o_dec, o_down, o_vec,
    W, gD, big, X, A, Tb, Q, O, X1, H, G, GP, X2, dZ, dX, dW, Zx, outg, inc, bias,
    tokb, r0, r1a, r1b, r2a, r2b, r3, r4, fin, decg, posr, vec, rv,
    ik, ek, yk, tk, ok, swk, agz, ag1, ag2, ag3, a2, a2b, rs0, rs1, rs2, rs3, rs4, rvk,
):
    dp = lax.axis_index("dp")
    f = lax.axis_index("fsdp")
    x = lax.rem(dp, 2)
    y = lax.rem(lax.div(dp, 2), 2)
    z = lax.div(dp, 4)
    sib = (dp, 1 - f)
    xn = (dp + 1 - 2 * x, f)
    yn = (dp + 2 - 4 * y, f)
    E = {}

    def zpeer(k):
        return lax.rem(z + k, NZ)

    def dev_z(k):
        return (lax.rem(dp + 4 * k, CHIPS), f)

    def peer(k):
        return (lax.rem(dp + k, CHIPS), f)

    def remote(src, dst, sems, idx, dev):
        c = pltpu.make_async_remote_copy(
            src_ref=src, dst_ref=dst, send_sem=sems.at[(0,) + idx], recv_sem=sems.at[(1,) + idx],
            device_id=dev, device_id_type=MESH,
        )
        c.start()
        return c

    def wait(copies):
        for c in copies:
            c.wait()

    flight = {}

    def gather(p, step):
        c0, a, n = GATHERS[p]
        if step > 0:
            wait(flight["g", p])
        if step == 0:
            part = W.at[f, z, y, x, :, c0 : c0 + n]
            cps = [remote(part, part, agz, (p, k - 1), dev_z(k)) for k in range(1, NZ)]
        elif step == 1:
            pa = W.at[f, :, y, x, :, c0 : c0 + a]
            pb = W.at[f, :, y, x, :, c0 + a : c0 + n]
            cps = [remote(pa, pa, ag1, (p, 0), yn), remote(pb, pb, ag1, (p, 1), xn)]
        elif step == 2:
            pa = W.at[f, :, :, x, :, c0 : c0 + a]
            pb = W.at[f, :, y, :, :, c0 + a : c0 + n]
            cps = [remote(pa, pa, ag2, (p, 0), xn), remote(pb, pb, ag2, (p, 1), yn)]
        elif step == 3:
            part = W.at[f, :, :, :, :, c0 : c0 + n]
            cps = [remote(part, part, ag3, (p,), sib)]
        else:
            cps = []
        flight["g", p] = cps

    def place(p, h, val):
        if p < 2:
            o_down[48 * p : 48 * p + 48, :] = val
        elif p == 2:
            decg[:, pl.ds(pl.multiple_of(256 * h, 128), 256)] = val
        elif p < 5:
            o_up[:, pl.ds(pl.multiple_of(1536 * h + 768 * (p - 3), 128), 768)] = val
        elif p == 5:
            o_out[:, pl.ds(pl.multiple_of(384 * h, 128), 384)] = val
        else:
            for i in range(3):
                at = pl.multiple_of(768 * i + 128 * (p - 6 + 3 * h), 128)
                o_qkv[:, pl.ds(at, 128)] = val[:, 128 * i : 128 * i + 128]

    def reduce(p, step):
        own, c0, a, w = SUMS[p]
        ref = gD if own else W
        b = w - a
        sl = p % SLOTS
        at = SUM_AT[p]
        if step > 0:
            wait(flight["r", p])
        cps = []
        if step == 0:
            cps = [remote(ref.at[1 - f, :, :, :, :, c0 : c0 + w], r0.at[p % 2, :, :, :, :, 0:w], rs0, (p,), sib)]
        elif step == 1:

            def add(i, carry):
                ref[f, i, :, :, :, c0 : c0 + w] = ref[f, i, :, :, :, c0 : c0 + w] + r0[p % 2, i, :, :, :, 0:w]
                return carry

            lax.fori_loop(0, NZ, add, 0)
            cps = [
                remote(ref.at[f, :, :, 1 - x, :, c0 : c0 + a], r1a.at[sl, :, :, :, 0:a], rs1, (p, 0), xn),
                remote(ref.at[f, :, 1 - y, :, :, c0 + a : c0 + w], r1b.at[sl, :, :, :, 0:b], rs1, (p, 1), yn),
            ]
        elif step == 2:

            def add(i, carry):
                ref[f, i, :, x, :, c0 : c0 + a] = ref[f, i, :, x, :, c0 : c0 + a] + r1a[sl, i, :, :, 0:a]
                ref[f, i, y, :, :, c0 + a : c0 + w] = ref[f, i, y, :, :, c0 + a : c0 + w] + r1b[sl, i, :, :, 0:b]
                return carry

            lax.fori_loop(0, NZ, add, 0)
            cps = [
                remote(ref.at[f, :, 1 - y, x, :, c0 : c0 + a], r2a.at[sl, :, :, 0:a], rs2, (p, 0), yn),
                remote(ref.at[f, :, y, 1 - x, :, c0 + a : c0 + w], r2b.at[sl, :, :, 0:b], rs2, (p, 1), xn),
            ]
        elif step == 3:

            def add(i, carry):
                ref[f, i, y, x, :, c0 : c0 + a] = ref[f, i, y, x, :, c0 : c0 + a] + r2a[sl, i, :, 0:a]
                ref[f, i, y, x, :, c0 + a : c0 + w] = ref[f, i, y, x, :, c0 + a : c0 + w] + r2b[sl, i, :, 0:b]
                return carry

            lax.fori_loop(0, NZ, add, 0)
            for k in range(1, NZ):
                src = ref.at[f, zpeer(k), y, x, :, c0 : c0 + w]
                cps.append(remote(src, r3.at[k - 1, :, at : at + w], rs3, (p, k - 1), dev_z(k)))
        elif step == 4:
            total = ref[f, z, y, x, :, c0 : c0 + w].astype(F32)
            for k in range(NZ - 1):
                total = total + r3[k, :, at : at + w].astype(F32)
            if own:
                place(p, None, total)
            else:
                fin[p % 2, :, 0:w] = total
                place(p, f, fin[p % 2, pl.ds(pl.multiple_of(24 * f, 8), 24), 0:w])
                src = fin.at[p % 2, pl.ds(pl.multiple_of(24 * (1 - f), 8), 24), 0:w]
                cps = [remote(src, r4.at[:, at - 1536 : at - 1536 + w], rs4, (p,), sib)]
        else:
            if not own:
                place(p, 1 - f, r4[:, at - 1536 : at - 1536 + w])
            finished(p)
        flight["r", p] = cps

    def scalars():
        E["filled"] = [[None] * CHIPS for _ in range(MICROS)]
        E["before"] = [[None] * CHIPS for _ in range(MICROS)]
        E["mine"], E["own"] = [], []
        for m in range(MICROS):
            running = jnp.int32(0)
            at_me = jnp.int32(0)
            for d in range(CHIPS):
                total = lens[m, 4 * d] + lens[m, 4 * d + 1] + lens[m, 4 * d + 2] + lens[m, 4 * d + 3]
                E["filled"][m][d] = total
                E["before"][m][d] = running
                at_me = at_me + jnp.where(dp == d, running, 0)
                running = running + total
            run, frun = jnp.int32(0), jnp.int32(0)
            ends, starts = [], []
            for c in range(4):
                n = lens[m, 4 * dp + c]
                run = run + n
                ends.append(run)
                starts.append(frun)
                for k in range(1, 5):
                    frun = frun + jnp.where(n >= 78 * k, 784, 0)
            E["mine"].append((at_me, run))
            E["own"].append((ends, starts, frun))

    def pick(m, d):
        lead = (dp - E["before"][m][d]) & (CHIPS - 1)
        first = (E["before"][m][d] + lead) >> 4
        return first, (E["filled"][m][d] - lead + CHIPS - 1) >> 4

    def pack(src, params):
        lane = _iota((16, RP), 1)
        sub = _iota((16, RP), 0)
        late = 16 + (sub & 3)
        for d in range(CHIPS):
            base, step, limit = params(d)
            want = base + step * sub
            O[16 * d : 16 * d + 16, 0:RP] = jnp.where((lane == want) & (want < limit), 1.0, 0.0).astype(BF)
            want = base + step * late
            O[256 + 16 * d : 272 + 16 * d, 0:RP] = jnp.where((lane == want) & (want < limit), 1.0, 0.0).astype(BF)
        head = _nn(O[0:256, 0:RP], src).astype(BF)
        third = (_iota((256, RP), 0) & 15) >> 2
        late_rows = O[256:512, 0:RP]
        rest = None
        for s in range(3):
            part = _nn(jnp.where(third == s, late_rows, jnp.zeros((), BF)), src[:, 256 * s : 256 * s + 256])
            rest = part if rest is None else rest + part
        return head, rest.astype(BF)

    def send_rows(m, src, params, sems):
        head, rest = pack(src, params)
        outg[m, :, :, 0:D] = head.reshape(CHIPS, 16, D)
        outg[m, :, :, D:PK] = rest.reshape(CHIPS, 16, PK - D)
        cps = []
        for k in range(1, CHIPS):
            to = peer(k)
            cps.append(remote(outg.at[m, to[0]], inc.at[m, dp], sems, (m, k - 1), to))
        inc[m, dp] = outg[m, dp]
        flight["a", m] = cps

    def rows(m):
        return slice(m * RP, (m + 1) * RP)

    def wt(h, c0, n):
        return W[h, :, :, :, :, c0 : c0 + n].reshape(D, n)

    def both(c0, n):
        return jnp.concatenate([wt(0, c0, n), wt(1, c0, n)], axis=1)

    def down_rows(q):
        return jnp.concatenate(
            [W[h, q, i // 2, i % 2, :, C_DOWN + 768 * k : C_DOWN + 768 * k + 768] for i in range(4) for h in range(2) for k in range(2)],
            axis=0,
        )

    def ln_parts(v):
        center = v - jnp.mean(v, axis=-1, keepdims=True)
        r = lax.rsqrt(jnp.mean(center * center, axis=-1, keepdims=True) + EPS)
        return center * r, r

    def ln_back(dh, xhat, r, gain):
        dxh = dh * gain
        return r * (dxh - jnp.mean(dxh, axis=-1, keepdims=True) - xhat * jnp.mean(dxh * xhat, axis=-1, keepdims=True))

    sub_p = _iota((RP, 1), 0)
    lane_p = _iota((1, RP), 1)

    sources = (i0, i1, i2, i3, i4, i5, i6, i7, i8, i9, i10)
    held = (w_qkv, w_out, w_up, w_dec, w_down, gain_a, gain_m, mask_tok, lens, vis, pos)
    made = {0: (o_qkv, e0), 1: (o_out, e1), 2: (o_up, e2), 3: (o_dec, e3), 4: (o_down, e4), 5: (o_vec, e5)}
    pending = {0: {6, 7, 8}, 1: {5}, 2: {3, 4}, 3: {2}, 4: {0, 1}}

    def emit(i):
        flight["e", i] = [pltpu.make_async_copy(*made[i], ek.at[i])]
        flight["e", i][0].start()

    def finished(p):
        for i, left in pending.items():
            if p in left:
                left.discard(p)
                if not left:
                    if i == 3:
                        o_dec[...] = decg[:, 0:DD]
                    emit(i)

    def begin():
        first = [pltpu.make_async_copy(a, b, ik.at[i]) for i, (a, b) in enumerate(zip(sources, held))]
        for c in first:
            c.start()
        bar = pltpu.get_barrier_semaphore()
        pl.semaphore_signal(bar, inc=1, device_id=sib, device_id_type=MESH)
        for k in range(1, CHIPS):
            pl.semaphore_signal(bar, inc=1, device_id=peer(k), device_id_type=MESH)
        E["tok"] = pltpu.make_async_copy(tok, tokb, tk.at[0])
        E["tok"].start()
        E["y"] = [pltpu.make_async_copy(cot.at[m], big.at[m * FULL : (m + 1) * FULL], yk.at[m]) for m in range(MICROS)]
        for c in E["y"]:
            c.start()
        wait(first)
        n = gain_a.shape[0]
        diag = _iota((n, n), 0) == _iota((n, n), 1)
        lane = _iota((n, 128), 1)

        def column(ref):
            return jnp.sum(jnp.where(diag, jnp.broadcast_to(ref[...].astype(F32)[None, :], (n, n)), 0.0), axis=1, keepdims=True)

        gains = jnp.where(lane == 0, column(gain_a), jnp.where(lane == 1, column(gain_m), 0.0)).astype(BF)
        for h in range(2):
            for p in range(3):
                for i in range(3):
                    j = p + 3 * h
                    c = C_QKV[p] + 128 * i
                    r3[h, 0:24, c : c + 128] = w_qkv[:, 768 * i + 128 * j : 768 * i + 128 * j + 128]
            r3[h, 0:24, C_OUT : C_OUT + 384] = w_out[:, 384 * h : 384 * h + 384]
            r3[h, 0:24, C_UP : C_UP + 1536] = w_up[:, 1536 * h : 1536 * h + 1536]
        r3[0, 0:24, C_DEC : C_DEC + 256] = w_dec[:, 0:256]
        r3[1, 0:24, C_DEC : C_DEC + 128] = w_dec[:, 256:384]
        r3[1, 0:24, C_DEC + 128 : C_DEC + 256] = gains
        W[f, z, y, x, :, C_DOWN : C_DOWN + 768] = w_down[0:CH, :]
        W[f, z, y, x, :, C_DOWN + 768 : C_ALL] = w_down[CH : 2 * CH, :]
        pl.semaphore_wait(bar, CHIPS)
        E["swap"] = remote(r3.at[1 - f, 0:32, 0:SWAPPED], r3.at[2, 0:32, 0:SWAPPED], swk, (0,), sib)
        scalars()

    def compose():
        E["swap"].wait()
        mine_rows = r3[f, 0:24, 0:SWAPPED].astype(F32)
        other_rows = r3[2, 0:24, 0:SWAPPED].astype(F32)
        lower = jnp.where(f == 0, mine_rows, other_rows)
        upper = jnp.where(f == 0, other_rows, mine_rows)
        W[f, z, y, x, :, 0:SWAPPED] = jnp.concatenate([lower, upper], axis=0).astype(BF)

    def load_tokens():
        E["tok"].wait()
        n = tokb.shape[0]
        for m in range(MICROS):
            A[m * RP + 304 : m * RP + 320, :] = jnp.zeros((16, D), BF)
            A[m * RP : m * RP + n, :] = tokb[:, m, :]

    def send_tokens(m):
        def params(d):
            first, count = pick(m, d)
            return first, 1, first + count

        send_rows(m, A[rows(m), :], params, a2)

    def layout():
        n = vis.shape[1]
        diag = _iota((RP, RP), 0) == _iota((RP, RP), 1)
        E["row"], E["col"] = [], []
        for m in range(MICROS):
            ends, starts, _ = E["own"][m]
            v = jnp.concatenate([vis[m : m + 1, :], jnp.zeros((1, RP - n), jnp.int32)], axis=1)

            def clip_of(p):
                return sum((jnp.where(p >= e, 1, 0) for e in ends))

            def start_of(cid):
                return sum((jnp.where(cid == c, starts[c], 0) for c in range(4)))

            cr, cc = clip_of(lane_p), clip_of(sub_p)
            bias[m] = jnp.where(cc == cr, 0.0, NEG).astype(BF)
            E["row"].append(jnp.where(cr < 4, start_of(cr) + v, -1))
            vcol = jnp.sum(jnp.where(diag, jnp.broadcast_to(v.astype(F32), (RP, RP)), 0.0), axis=1, keepdims=True)
            E["col"].append(jnp.where(cc < 4, start_of(cc) + vcol.astype(jnp.int32), -1))
            for c in range(FULL // EC):
                posr[m, c : c + 1, :] = pos[m : m + 1, c * EC : (c + 1) * EC]

    def project_back(m):
        E["y"][m].wait()
        full_total = E["own"][m][2]
        extra = sub_p == RP - 1
        target = E["col"][m]

        def chunk(c, acc):
            spot = _iota((RP, YC), 1) + c * YC
            hit = (spot == target) | (extra & (spot < full_total))
            ys = big[pl.ds(pl.multiple_of(m * FULL + c * YC, 64), YC), :]
            return acc + _nn(jnp.where(hit, 1.0, 0.0).astype(BF), ys)

        acc = lax.fori_loop(0, FULL // YC, chunk, jnp.zeros((RP, DD), F32))
        whole = jnp.sum(jnp.where(extra, acc, 0.0), axis=0, keepdims=True)
        acc = jnp.where(extra, 0.0, acc)
        dZ[rows(m), :] = acc.astype(BF)
        s = whole - jnp.sum(acc, axis=0, keepdims=True)
        E["mask"] = s if m == 0 else E["mask"] + s

    def blocks(m):
        wait(flight["a", m])
        off, count = E["mine"][m]

        def source(p):
            return jnp.where(p < count, ((off + p) & (CHIPS - 1)) * 16, -4096)

        p = sub_p[0:256]
        hit = jnp.where(_iota((256, 256), 1) == source(p) + (p >> 4), 1.0, 0.0).astype(BF)
        got = inc[m].reshape(256, PK)
        X[m * RP : m * RP + 256, :] = _nn(hit, got[:, 0:D]).astype(BF)
        p = sub_p[0:64] + 256
        for s in range(3):
            hit = jnp.where(_iota((64, 256), 1) == source(p) + 4 * s + (p >> 4) - 16, 1.0, 0.0).astype(BF)
            X[m * RP + 256 : m * RP + RP, 256 * s : 256 * s + 256] = _nn(hit, got[:, D:PK]).astype(BF)

    def gains():
        g = jnp.transpose(wt(1, C_DEC + 128, 128).astype(F32))
        E["gain_attn"], E["gain_mlp"] = g[0:1, :], g[1:2, :]
        E["gsum_attn"] = E["gsum_mlp"] = None

    def ln1(m):
        xhat, _ = ln_parts(X[rows(m), :].astype(F32))
        A[rows(m), :] = (xhat * E["gain_attn"]).astype(BF)

    def qkv(p, m):
        res = _nn(A[rows(m), :], both(C_QKV[p], 384)).astype(BF)
        Q[rows(m), 384 * p : 384 * p + 384] = res[:, 0:384]
        Q[rows(m), 384 * p + 1152 : 384 * p + 1536] = res[:, 384:768]

    lane128 = _iota((1, 128), 1)
    head_mask = (lane128 < 64, lane128 >= 64)
    QB = ((0, 128), (128, 128), (256, 64))

    def attend(p, m):
        r = rows(m)

        def pair(i, carry):
            j = p + 3 * i
            at = pl.multiple_of(j * 384, 128)
            q2, k2, v2 = (Q[r, pl.ds(pl.multiple_of(at + 128 * k, 128), 128)] for k in range(3))
            v_t = jnp.transpose(v2)
            for b0, bn in QB:
                halves = []
                for h in range(2):
                    qm = jnp.where(head_mask[h], q2[b0 : b0 + bn], jnp.zeros((), BF))
                    s = _nt(k2, qm) * 0.125 + bias[m, :, b0 : b0 + bn].astype(F32)
                    e = jnp.exp(s - jnp.max(s, axis=0, keepdims=True))
                    pb = (e * (1.0 / jnp.sum(e, axis=0, keepdims=True))).astype(BF)
                    big[pl.ds(pl.multiple_of((m * 12 + 2 * j + h) * RP, 64), RP), b0 : b0 + bn] = pb
                    halves.append(_nn(v_t[64 * h : 64 * h + 64], pb))
                O[m * RP + b0 : m * RP + b0 + bn, pl.ds(pl.multiple_of(j * 128, 128), 128)] = jnp.transpose(jnp.concatenate(halves, axis=0)).astype(BF)
            return carry

        lax.fori_loop(0, 2, pair, 0)

    def attend_back(p, m):
        r = rows(m)

        def pair(i, carry):
            j = p + 3 * i
            at = pl.multiple_of(j * 384, 128)
            cq, ck, cv = (pl.ds(pl.multiple_of(at + 128 * k, 128), 128) for k in range(3))
            q2, k2, v2 = Q[r, cq], Q[r, ck], Q[r, cv]
            do2 = X2[r, pl.ds(pl.multiple_of(j * 128, 128), 128)]
            k_t = jnp.transpose(k2)
            dk = jnp.zeros((RP, 128), F32)
            dv = jnp.zeros((RP, 128), F32)
            for b0, bn in QB:
                halves = []
                for h in range(2):
                    dom = jnp.where(head_mask[h], do2[b0 : b0 + bn], jnp.zeros((), BF))
                    qm = jnp.where(head_mask[h], q2[b0 : b0 + bn], jnp.zeros((), BF))
                    dp_t = _nt(v2, dom)
                    pb = big[pl.ds(pl.multiple_of((m * 12 + 2 * j + h) * RP, 64), RP), b0 : b0 + bn]
                    pf = pb.astype(F32)
                    w = pf * dp_t
                    ds = (w - pf * jnp.sum(w, axis=0, keepdims=True)).astype(BF)
                    halves.append(_nn(k_t[64 * h : 64 * h + 64], ds))
                    dv = dv + _nn(pb, dom)
                    dk = dk + _nn(ds, qm)
                dq = jnp.transpose(jnp.concatenate(halves, axis=0)) * 0.125
                Q[m * RP + b0 : m * RP + b0 + bn, cq] = dq.astype(BF)
            Q[r, ck] = (dk * 0.125).astype(BF)
            Q[r, cv] = dv.astype(BF)
            return carry

        lax.fori_loop(0, 2, pair, 0)

    def after_attention(m):
        x1 = X[rows(m), :].astype(F32) + _nn(O[rows(m), :], both(C_OUT, 384))
        X1[rows(m), :] = x1
        xhat, _ = ln_parts(x1)
        H[rows(m), :] = (xhat * E["gain_mlp"]).astype(BF)

    def up(b, h):
        w = wt(h, C_UP + 768 * b, 768)
        c0 = 1536 * h + 768 * b

        def body(m, carry):
            at = pl.ds(pl.multiple_of(m * RP, RP), RP)
            u = _nn(H[at, :], w)
            cdf = 0.5 * (1.0 + lax.erf(u * (1.0 / math.sqrt(2.0))))
            pdf = jnp.exp(u * u * -0.5) * (1.0 / math.sqrt(2.0 * math.pi))
            G[at, c0 : c0 + 768] = (u * cdf).astype(BF)
            GP[at, c0 : c0 + 768] = (cdf + u * pdf).astype(BF)
            return carry

        lax.fori_loop(0, MICROS, body, 0)

    def dec_weights():
        return jnp.concatenate([wt(0, C_DEC, 256), wt(1, C_DEC, 128)], axis=1)

    def back_dec():
        w = dec_weights()
        for m in range(MICROS):
            d = _nt(dZ[rows(m), :], w)
            dX[rows(m), :] = d
            dW[rows(m), :] = d.astype(BF)

    def put_grad(ref, h, c0, n, val):
        ref[h, :, :, :, :, c0 : c0 + n] = val.astype(BF).reshape(NZ, NY, NX, CH, n)

    def grad_down(q):
        val = _tn(G[:, 768 * q : 768 * q + 768], dW[...]).astype(BF)
        for i in range(4):
            for h in range(2):
                for k in range(2):
                    n = 4 * i + 2 * h + k
                    gD[h, q, i // 2, i % 2, :, 768 * k : 768 * k + 768] = val[48 * n : 48 * n + 48, :]

    def after_mlp(m):
        acc = X1[rows(m), :]
        for q in range(4):
            acc = acc + _nn(G[rows(m), 768 * q : 768 * q + 768], down_rows(q))
        X2[rows(m), :] = acc.astype(BF)

    def project():
        w = dec_weights()
        for m in range(MICROS):
            Zx[rows(m), 0:DD] = _nn(X2[rows(m), :], w).astype(BF)
            Zx[rows(m), DD:512] = jnp.ones((RP, 128), BF)
        gd = _tn(X2[...], dZ[...])
        put_grad(W, 0, C_DEC, 256, gd[:, 0:256])
        put_grad(W, 1, C_DEC, 128, gd[:, 256:384])

    def back_down(q):
        w = down_rows(q)
        for m in range(MICROS):
            back = _nt(dW[rows(m), :], w)
            at = slice(768 * q, 768 * q + 768)
            GP[rows(m), at] = (back * GP[rows(m), at].astype(F32)).astype(BF)

    def grad_up(b):
        if b == 0:
            Tb[...] = jnp.transpose(H[...])
        for h in range(2):
            c0 = 1536 * h + 768 * b
            put_grad(W, h, C_DOWN + 768 * b, 768, _nn(Tb[...], GP[:, c0 : c0 + 768]))

    def back_up(m):
        dh = _nt(GP[rows(m), 0:1536], wt(0, C_UP, 1536)) + _nt(GP[rows(m), 1536:3072], wt(1, C_UP, 1536))
        xhat, r = ln_parts(X1[rows(m), :])
        s = jnp.sum(dh * xhat, axis=0, keepdims=True)
        E["gsum_mlp"] = s if m == 0 else E["gsum_mlp"] + s
        dx1 = dX[rows(m), :] + ln_back(dh, xhat, r, E["gain_mlp"])
        dX[rows(m), :] = dx1
        dW[rows(m), :] = dx1.astype(BF)

    def back_out():
        w = both(C_OUT, 384)
        for m in range(MICROS):
            X2[rows(m), :] = _nt(dW[rows(m), :], w).astype(BF)
        go = _tn(O[...], dW[...])
        put_grad(W, 0, C_OUT, 384, go[:, 0:384])
        put_grad(W, 1, C_OUT, 384, go[:, 384:768])

    def back_qkv(m):
        da = None
        for h in range(2):
            w = jnp.concatenate([wt(h, C_QKV[p], 384) for p in range(3)], axis=1)
            part = _nt(Q[rows(m), 1152 * h : 1152 * h + 1152], w)
            da = part if da is None else da + part
        xhat, r = ln_parts(X[rows(m), :].astype(F32))
        s = jnp.sum(da * xhat, axis=0, keepdims=True)
        E["gsum_attn"] = s if m == 0 else E["gsum_attn"] + s
        H[rows(m), :] = (dX[rows(m), :] + ln_back(da, xhat, r, E["gain_attn"])).astype(BF)

    def return_rows(m):
        off, count = E["mine"][m]

        def params(d):
            return (d - off) & (CHIPS - 1), CHIPS, count

        send_rows(m, H[rows(m), :], params, a2b)

    def grad_qkv(p):
        if p == 0:
            X2_t = jnp.transpose(A[...])
            Tb[...] = X2_t
        val = _nn(Tb[...], jnp.concatenate([Q[:, 384 * p : 384 * p + 384], Q[:, 384 * p + 1152 : 384 * p + 1536]], axis=1))
        put_grad(W, 0, C_UP + 384 * p, 384, val[:, 0:384])
        put_grad(W, 1, C_UP + 384 * p, 384, val[:, 384:768])

    def tables():
        chan = _iota((64, DD), 1)
        even = (chan & 1) == 0
        rate = jnp.exp((chan - (chan & 1)).astype(F32) * (-math.log(10000.0) / DD))
        ang = (32 * _iota((64, DD), 0)).astype(F32) * rate
        sa, ca = jnp.sin(ang), jnp.cos(ang)
        angb = _iota((64, DD), 0).astype(F32) * rate
        sb, cb = jnp.sin(angb), jnp.cos(angb)
        GP[0:256, 0 : 4 * DD] = jnp.zeros((256, 4 * DD), BF)

        def put(at, col, val):
            hi = val.astype(BF)
            GP[at : at + 64, col : col + DD] = hi
            GP[128 + at : 192 + at, col : col + DD] = (val - hi.astype(F32)).astype(BF)

        put(0, 0, jnp.where(even, sa, ca))
        put(0, DD, jnp.where(even, ca, -sa))
        put(64, 2 * DD, cb)
        put(64, 3 * DD, sb)

    def decode(m, lo, hi):
        full_total = E["own"][m][2]
        target = E["row"][m]
        mt = mask_tok[...].astype(F32)[None, :]

        def chunk(c, carry):
            spot = _iota((EC, RP), 0) + c * EC
            hit = jnp.where(spot == target, 1.0, 0.0).astype(BF)
            mz = _nn(hit, Zx[rows(m), :])
            ps = posr[m, pl.ds(c, 1), :]
            kk = _iota((256, EC), 0) & 127
            want = jnp.where(kk < 64, ps >> 5, (ps & 31) + 64)
            code = _tn(jnp.where(kk == want, 1.0, 0.0).astype(BF), GP[0:256, 0 : 4 * DD])
            pe = code[:, 0:DD] * code[:, 2 * DD : 3 * DD] + code[:, DD : 2 * DD] * code[:, 3 * DD : 4 * DD]
            live = jnp.where(_iota((EC, 1), 0) + c * EC < full_total, 1.0, 0.0)
            cov = jnp.concatenate([mz[:, DD:512]] * 3, axis=1)
            val = mz[:, 0:DD] + (live - cov) * mt + live * pe
            big[pl.ds(pl.multiple_of(m * FULL + c * EC, 32), EC), :] = val.astype(BF)
            return carry

        lax.fori_loop(lo, hi, chunk, 0)
        if hi == FULL // EC:
            c = pltpu.make_async_copy(big.at[m * FULL : (m + 1) * FULL], o_rows.at[m], ok.at[m])
            c.start()
            flight["d", m] = [c]

    def collect(m):
        wait(flight["a", m])
        lane = _iota((1, 256), 1)
        early = jnp.full((1, 256), -1, jnp.int32)
        late = jnp.full((1, 256), -1, jnp.int32)
        for d in range(CHIPS):
            first, count = pick(m, d)
            s = lane - 16 * d
            here = (s >= 0) & (s < 16)
            early = jnp.where(here & (s < count), first + s, early)
            t = 16 + (s & 3)
            late = jnp.where(here & (t < count), first + t, late)
        got = inc[m].reshape(256, PK)
        row = _iota((RP, 256), 0)
        head = _nn(jnp.where(row == early, 1.0, 0.0).astype(BF), got[:, 0:D])
        third = (lane & 15) >> 2
        parts = []
        for s in range(3):
            hit = jnp.where((row == late) & (third == s), 1.0, 0.0).astype(BF)
            parts.append(head[:, 256 * s : 256 * s + 256] + _nn(hit, got[:, D:PK]))
        back = jnp.concatenate(parts, axis=1).astype(BF)
        tokb[:, m, :] = back[0 : tokb.shape[0]]

    def vector(step):
        if step > 0:
            wait(flight["v"])
        if step == 0:
            ga, gm = E["gsum_attn"], E["gsum_mlp"]
            vec[...] = jnp.concatenate(
                [E["mask"], ga[:, 0:DD], ga[:, DD:D], gm[:, 0:DD], gm[:, DD:D], jnp.zeros((3, DD), F32)], axis=0
            )
        elif step < 4:
            vec[...] = vec[...] + rv[step - 1]
        if step < 3:
            flight["v"] = [remote(vec, rv.at[step], rvk, (step,), (sib, xn, yn)[step])]
        elif step == 3:
            flight["v"] = [remote(vec, rv.at[2 + k], rvk, (2 + k,), dev_z(k)) for k in range(1, NZ)]
        else:
            o_vec[...] = vec[...] + rv[3] + rv[4] + rv[5]
            emit(5)

    def end():
        c = pltpu.make_async_copy(tokb, o_tok, tk.at[0])
        c.start()
        c.wait()
        for i in range(6):
            wait(flight["e", i])
        wait(flight["d", 0])
        wait(flight["d", 1])

    steps = {
        S_BEGIN: begin, S_COMPOSE: compose, S_LOAD: load_tokens, S_SEND: send_tokens, S_LAYOUT: layout, S_PROJ: project_back,
        S_BLOCKS: blocks, S_GAINS: gains, S_LN1: ln1, S_QKV: qkv, S_ATT: attend, S_X1: after_attention, S_UP: up, S_BDEC: back_dec,
        S_GDOWN: grad_down, S_X2: after_mlp, S_Z: project, S_BDOWN: back_down, S_GUP: grad_up, S_BUP: back_up, S_BOUT: back_out,
        S_ATTB: attend_back, S_BQKV: back_qkv, S_RET: return_rows, S_GQKV: grad_qkv, S_TAB: tables, S_DEC: decode, S_COLL: collect,
        S_VEC: vector, S_END: end, S_G: gather, S_R: reduce,
    }
    for name, *args in ORDER:
        steps[name](*args)


ORDER = (
    (S_BEGIN,), (S_COMPOSE,), (S_G, 2, 0), (S_G, 1, 0), (S_G, 0, 0), (S_LOAD,), (S_SEND, 1), (S_G, 4, 0), (S_G, 3, 0),
    (S_G, 1, 1), (S_G, 5, 0), (S_G, 2, 1), (S_G, 2, 2), (S_G, 0, 1), (S_SEND, 0), (S_G, 1, 2), (S_LAYOUT,), (S_G, 0, 2),
    (S_G, 2, 3), (S_G, 1, 3), (S_PROJ, 0), (S_G, 1, 4), (S_G, 4, 1), (S_G, 6, 0), (S_PROJ, 1), (S_G, 2, 4), (S_BLOCKS, 1),
    (S_G, 0, 3), (S_G, 0, 4), (S_GAINS,), (S_G, 3, 1), (S_LN1, 1), (S_QKV, 0, 1), (S_G, 7, 0), (S_G, 4, 2), (S_G, 5, 1),
    (S_QKV, 1, 1), (S_BDEC,), (S_ATT, 1, 1), (S_ATT, 0, 1), (S_G, 3, 2), (S_QKV, 2, 1), (S_ATT, 2, 1), (S_BLOCKS, 0),
    (S_LN1, 0), (S_QKV, 2, 0), (S_QKV, 0, 0), (S_QKV, 1, 0), (S_G, 5, 2), (S_G, 4, 3), (S_ATT, 2, 0), (S_G, 3, 3),
    (S_ATT, 0, 0), (S_G, 6, 1), (S_ATT, 1, 0), (S_G, 3, 4), (S_X1, 1), (S_G, 5, 3), (S_X1, 0), (S_G, 7, 1), (S_G, 4, 4),
    (S_UP, 0, 1), (S_G, 6, 2), (S_G, 5, 4), (S_UP, 0, 0), (S_UP, 1, 1), (S_G, 7, 2), (S_UP, 1, 0), (S_GDOWN, 0), (S_GDOWN, 2),
    (S_GDOWN, 3), (S_GDOWN, 1), (S_R, 0, 0), (S_G, 6, 3), (S_R, 0, 1), (S_R, 1, 0), (S_G, 6, 4), (S_G, 7, 3), (S_R, 1, 1),
    (S_G, 7, 4), (S_BDOWN, 0), (S_X2, 0), (S_BDOWN, 2), (S_X2, 1), (S_Z,), (S_R, 2, 0), (S_BDOWN, 3), (S_R, 0, 2),
    (S_R, 2, 1), (S_BDOWN, 1), (S_GUP, 0), (S_R, 1, 2), (S_R, 3, 0), (S_GUP, 1), (S_R, 0, 3), (S_R, 2, 2), (S_R, 3, 1),
    (S_R, 4, 0), (S_BUP, 0), (S_R, 1, 3), (S_BUP, 1), (S_BOUT,), (S_ATTB, 2, 0), (S_R, 3, 2), (S_R, 0, 4), (S_R, 4, 1),
    (S_R, 5, 0), (S_R, 2, 3), (S_ATTB, 0, 0), (S_R, 5, 1), (S_R, 3, 3), (S_ATTB, 1, 0), (S_BQKV, 0), (S_R, 4, 2), (S_RET, 0),
    (S_ATTB, 0, 1), (S_GQKV, 0), (S_R, 5, 2), (S_R, 6, 0), (S_ATTB, 1, 1), (S_GQKV, 1), (S_R, 6, 1), (S_R, 7, 0), (S_R, 4, 3),
    (S_ATTB, 2, 1), (S_BQKV, 1), (S_VEC, 0), (S_R, 7, 1), (S_RET, 1), (S_R, 3, 4), (S_GQKV, 2), (S_R, 8, 0), (S_R, 2, 4),
    (S_R, 0, 5), (S_R, 5, 3), (S_TAB,), (S_R, 6, 2), (S_R, 8, 1), (S_R, 1, 4), (S_R, 3, 5), (S_DEC, 0, 0, 7), (S_VEC, 1),
    (S_R, 7, 2), (S_DEC, 1, 0, 7), (S_R, 1, 5), (S_R, 6, 3), (S_VEC, 2), (S_R, 2, 5), (S_R, 4, 4), (S_R, 8, 2), (S_R, 7, 3),
    (S_DEC, 1, 7, 14), (S_R, 8, 3), (S_R, 5, 4), (S_R, 4, 5), (S_R, 6, 4), (S_VEC, 3), (S_DEC, 0, 7, 14), (S_R, 5, 5),
    (S_R, 7, 4), (S_R, 6, 5), (S_R, 8, 4), (S_COLL, 1), (S_COLL, 0), (S_R, 7, 5), (S_VEC, 4), (S_R, 8, 5), (S_END,),
)


def _mega_call(tok, w_qkv, w_out, w_up, w_dec, w_down, gain_a, gain_m, mask_tok, lens, vis, pos, cot):
    vm = lambda *s: pltpu.VMEM(s[:-1], s[-1])
    sem = lambda *s: pltpu.SemaphoreType.DMA(s)
    ANY = pl.BlockSpec(memory_space=pl.ANY)
    raw = (w_qkv, w_out, w_up, w_dec, w_down, gain_a, gain_m, mask_tok, lens, vis, pos)
    grads = [jax.ShapeDtypeStruct(w.shape, F32) for w in raw[:5]] + [jax.ShapeDtypeStruct((8, DD), F32)]
    held = [(pltpu.SMEM if a is lens else pltpu.VMEM)(a.shape, a.dtype) for a in raw] + [pltpu.VMEM(a.shape, F32) for a in grads]
    scratch = [
        vm(2, NZ, NY, NX, CH, C_ALL, BF),
        vm(2, NZ, NY, NX, CH, 1536, BF),
        vm(24 * RP, DD, BF),
        vm(RT, D, BF),
        vm(RT, D, BF),
        vm(D, RT, BF),
        vm(RT, 3 * D, BF),
        vm(RT, D, BF),
        vm(RT, D, F32),
        vm(RT, D, BF),
        vm(RT, 4 * D, BF),
        vm(RT, 4 * D, BF),
        vm(RT, D, BF),
        vm(RT, DD, BF),
        vm(RT, D, F32),
        vm(RT, D, BF),
        vm(RT, 512, BF),
        vm(MICROS, CHIPS, 16, PK, BF),
        vm(MICROS, CHIPS, 16, PK, BF),
        vm(MICROS, RP, RP, BF),
        pltpu.VMEM(tok.shape, BF),
        vm(2, NZ, NY, NX, CH, 768, BF),
        vm(SLOTS, NZ, 2, CH, 384, BF),
        vm(SLOTS, NZ, 2, CH, 384, BF),
        vm(SLOTS, NZ, CH, 384, BF),
        vm(SLOTS, NZ, CH, 384, BF),
        vm(NZ - 1, CH, C_ALL, BF),
        vm(24, SWAPPED, F32),
        vm(2, CH, 768, F32),
        vm(24, 512, F32),
        vm(MICROS, FULL // EC, EC, jnp.int32),
        vm(8, DD, F32),
        vm(6, 8, DD, F32),
    ]
    sems = [
        sem(11), sem(6), sem(2), sem(1), sem(2), sem(2, 1), sem(2, 8, 3), sem(2, 8, 2), sem(2, 8, 2), sem(2, 8), sem(2, 2, 15), sem(2, 2, 15),
        sem(2, 9), sem(2, 9, 2), sem(2, 9, 2), sem(2, 9, 3), sem(2, 9), sem(2, 6),
    ]
    out = pl.pallas_call(
        _mega,
        out_shape=[jax.ShapeDtypeStruct(cot.shape, BF), jax.ShapeDtypeStruct(tok.shape, BF)] + grads,
        in_specs=[ANY] * 13,
        out_specs=[ANY] * 8,
        scratch_shapes=held + scratch + sems,
        compiler_params=pltpu.CompilerParams(collective_id=0, has_side_effects=True, vmem_limit_bytes=VMEM_BYTES),
    )(tok, *raw, cot)
    return out


VMEM_BYTES = 63 * 2**20


def _hand_over(*refs):
    ins, outs, o_ga, o_gm, o_mask = refs[:8], refs[8:15], refs[15], refs[16], refs[17]
    bufs, vbuf, in_sem, out_sem = refs[18:25], refs[25], refs[26], refs[27]
    parts = ins[0].shape[1] // 4
    pieces = [(0, (m, slice(i * parts, (i + 1) * parts))) for m in range(MICROS) for i in range(4)]
    pieces += [(k, (slice(None),)) for k in range(1, 7)]
    load = pltpu.make_async_copy(ins[7], vbuf, in_sem.at[len(pieces)])
    load.start()
    loads = [pltpu.make_async_copy(ins[k].at[at], bufs[k].at[at], in_sem.at[i]) for i, (k, at) in enumerate(pieces)]
    stores = [pltpu.make_async_copy(bufs[k].at[at], outs[k].at[at], out_sem.at[i]) for i, (k, at) in enumerate(pieces)]
    for c in loads:
        c.start()
    load.wait()
    n = o_ga.shape[0]
    me = lax.axis_index("dp") * 2 + lax.axis_index("fsdp")
    v = vbuf[...]
    for i, o in ((1, o_ga), (3, o_gm)):
        row = jnp.concatenate([v[i : i + 1], v[i + 1 : i + 2]], axis=1)
        turned = pltpu.roll(jnp.broadcast_to(row, (8, D)), D - n * me, 1)
        o[...] = turned[0:1, 0:n].reshape(n)
    o_mask[...] = v[0:1].reshape(DD)
    for c, d in zip(loads, stores):
        c.wait()
        d.start()
    for d in stores:
        d.wait()


def _hand_over_call(n, *arrays):
    V = pl.BlockSpec(memory_space=pltpu.VMEM)
    ANY = pl.BlockSpec(memory_space=pl.ANY)
    like = lambda a: jax.ShapeDtypeStruct(a.shape, a.dtype)
    flat = lambda k: jax.ShapeDtypeStruct((k,), F32)
    return pl.pallas_call(
        _hand_over,
        out_shape=[like(a) for a in arrays[:7]] + [flat(n), flat(n), flat(DD)],
        in_specs=[ANY] * 8,
        out_specs=[ANY] * 7 + [V] * 3,
        scratch_shapes=[pltpu.VMEM(a.shape, a.dtype) for a in arrays]
        + [pltpu.SemaphoreType.DMA((15,)), pltpu.SemaphoreType.DMA((14,))],
        compiler_params=pltpu.CompilerParams(vmem_limit_bytes=VMEM_BYTES),
    )(*arrays)


def per_device_fused(
    tokens, gain_attn, gain_mlp, w_qkv, w_out, w_up, w_down, w_dec, mask_token, clip_lengths, vis_index, pos_index, cotangent,
):
    tok = jnp.transpose(tokens[0], (1, 0, 2))
    made = _mega_call(
        tok, w_qkv, w_out, w_up, w_dec, w_down, gain_attn, gain_mlp, mask_token,
        clip_lengths[0], vis_index[0], pos_index[0], cotangent[0],
    )
    rows_out, returned, g_qkv, g_out, g_up, g_dec, g_down, ga, gm, mask = _hand_over_call(gain_attn.shape[0], *made)
    returned = jnp.transpose(returned, (1, 0, 2))
    return (rows_out[None], returned[None], ga, gm, g_qkv, g_out, g_up, g_down, g_dec, mask)

def solution(mesh):
    in_specs = (
        P("fsdp", None, "dp", None),
        P(("dp", "fsdp")),
        P(("dp", "fsdp")),
        P(("dp", "fsdp"), None),
        P(("dp", "fsdp"), None),
        P(("dp", "fsdp"), None),
        P(("dp", "fsdp"), None),
        P(("dp", "fsdp"), None),
        P(),
        P("fsdp", None, None),
        P("fsdp", None, "dp"),
        P("fsdp", None, "dp"),
        P("fsdp", None, "dp", None),
    )
    out_specs = (
        P("fsdp", None, "dp", None),
        P("fsdp", None, "dp", None),
        P(("dp", "fsdp")),
        P(("dp", "fsdp")),
        P(("dp", "fsdp"), None),
        P(("dp", "fsdp"), None),
        P(("dp", "fsdp"), None),
        P(("dp", "fsdp"), None),
        P(("dp", "fsdp"), None),
        P(),
    )
    body = per_device_fused if mesh.shape["dp"] == CHIPS and mesh.shape["fsdp"] == 2 else per_device
    return jax.shard_map(
        body, mesh=mesh, in_specs=in_specs, out_specs=out_specs, check_vma=False
    )
```

```python
import math

import jax
import jax.numpy as jnp
from jax import lax
from jax.experimental import pallas as pl
from jax.experimental.pallas import tpu as pltpu
from jax.sharding import PartitionSpec as P

HEADS = 12
HEAD = 64
SHORT = 78
FULL_UNIT = 784


NEG = -1e30
EPS = 1e-06


def layer_norm(values, scale_gain):
    center = values - jnp.mean(values, axis=-1, keepdims=True)
    spread = jnp.mean(center * center, axis=-1, keepdims=True)
    return center * lax.rsqrt(spread + EPS) * scale_gain


def softmax_rows(scores):
    shifted = scores - jnp.max(scores, axis=-1, keepdims=True)
    powers = jnp.exp(shifted)
    return powers / jnp.sum(powers, axis=-1, keepdims=True)


def gelu_exact(values):
    return 0.5 * values * (1.0 + lax.erf(values * (1.0 / math.sqrt(2.0))))


def sinusoid(table_index, features):
    channel = jnp.arange(features)
    rates = jnp.exp((channel // 2 * 2).astype(jnp.float32) * (-math.log(10000.0) / features))
    angles = table_index.astype(jnp.float32)[:, None] * rates[None, :]
    return jnp.where(channel % 2 == 0, jnp.sin(angles), jnp.cos(angles))


def block_layout(lengths, row_count):
    clip_ends = jnp.cumsum(lengths)
    full_sizes = lengths // SHORT * FULL_UNIT
    full_ends = jnp.cumsum(full_sizes)
    full_starts = full_ends - full_sizes
    row_ids = jnp.arange(row_count)
    clip_of = jnp.sum((row_ids[:, None] >= clip_ends[None, :]).astype(jnp.int32), axis=1)
    live_rows = clip_of < lengths.shape[0]
    slot_ids = jnp.arange(lengths.shape[0])
    start_of = jnp.sum(
        jnp.where(clip_of[:, None] == slot_ids[None, :], full_starts[None, :], 0), axis=1
    )
    return (clip_of, live_rows, start_of, full_ends[-1])


def contract(left_side, right_side, pattern):
    return jnp.einsum(pattern, left_side, right_side, preferred_element_type=jnp.float32)


def layer_pass(block_in, lengths, visible, position, grad_rows, params, mask_token):
    gain_attn, gain_mlp, w_qkv, w_out, w_up, w_down, w_dec = params
    row_count = block_in.shape[0]
    features = block_in.shape[1]
    full_count = grad_rows.shape[0]
    clip_of, live_rows, start_of, total_full = block_layout(lengths, row_count)
    same_clip = clip_of[:, None] == clip_of[None, :]
    inputs = block_in.astype(jnp.float32)
    normed, norm_attn_back = jax.vjp(layer_norm, inputs, gain_attn.astype(jnp.float32))
    normed = normed.astype(jnp.bfloat16)
    mixed_qkv = contract(normed, w_qkv, "pc,ce->pe").astype(jnp.bfloat16)
    queries = mixed_qkv[:, :features].reshape(row_count, HEADS, HEAD)
    key_rows = mixed_qkv[:, features : 2 * features].reshape(row_count, HEADS, HEAD)
    value_rows = mixed_qkv[:, 2 * features :].reshape(row_count, HEADS, HEAD)
    scores = contract(queries, key_rows, "qhd,khd->hqk") * HEAD ** (-0.5)
    scores = jnp.where(same_clip[None], scores, NEG)
    weights, soft_back = jax.vjp(softmax_rows, scores)
    weights_low = weights.astype(jnp.bfloat16)
    attended = (
        contract(weights_low, value_rows, "hqk,khd->qhd")
        .reshape(row_count, features)
        .astype(jnp.bfloat16)
    )
    after_attn = inputs + contract(attended, w_out, "pc,ce->pe")
    hidden, norm_mlp_back = jax.vjp(layer_norm, after_attn, gain_mlp.astype(jnp.float32))
    hidden = hidden.astype(jnp.bfloat16)
    upward = contract(hidden, w_up, "pc,cf->pf")
    activated, gelu_back = jax.vjp(gelu_exact, upward)
    activated = activated.astype(jnp.bfloat16)
    after_mlp = after_attn + contract(activated, w_down, "pf,fc->pc")
    final_low = after_mlp.astype(jnp.bfloat16)
    projected = contract(final_low, w_dec, "pc,ce->pe").astype(jnp.bfloat16)
    full_index = jnp.arange(full_count)
    target = start_of + visible
    place_map = ((full_index[:, None] == target[None, :]) & live_rows[None, :]).astype(jnp.bfloat16)
    covered = jnp.sum(place_map, axis=1, dtype=jnp.float32)
    full_live = (full_index < total_full).astype(jnp.float32)
    masked_share = full_live - covered
    decoded = (
        contract(place_map, projected, "ip,pe->ie")
        + masked_share[:, None] * mask_token.astype(jnp.float32)[None, :]
        + full_live[:, None] * sinusoid(position, projected.shape[1])
    )
    grad_full = grad_rows.astype(jnp.float32)
    mask_term = jnp.sum(masked_share[:, None] * grad_full, axis=0)
    back_proj = contract(place_map, grad_rows, "ip,ie->pe").astype(jnp.bfloat16)
    grad_dec = contract(final_low, back_proj, "pc,pe->ce")
    back_final = contract(back_proj, w_dec, "pe,ce->pc")
    back_mlp = back_final.astype(jnp.bfloat16)
    grad_down = contract(activated, back_mlp, "pf,pc->fc")
    back_act = contract(back_mlp, w_down, "pc,fc->pf")
    back_up = gelu_back(back_act)[0].astype(jnp.bfloat16)
    grad_up = contract(hidden, back_up, "pc,pf->cf")
    back_hidden = contract(back_up, w_up, "pf,cf->pc")
    back_norm_mlp, grad_gain_mlp = norm_mlp_back(back_hidden)
    back_after = back_final + back_norm_mlp
    back_attn_out = back_after.astype(jnp.bfloat16)
    grad_out = contract(attended, back_attn_out, "pc,pe->ce")
    back_attended = (
        contract(back_attn_out, w_out, "pe,ce->pc")
        .astype(jnp.bfloat16)
        .reshape(row_count, HEADS, HEAD)
    )
    back_weights = contract(back_attended, value_rows, "qhd,khd->hqk")
    back_values = contract(weights_low, back_attended, "hqk,qhd->khd")
    back_scores = soft_back(back_weights)[0].astype(jnp.bfloat16) * HEAD ** (-0.5)
    back_queries = contract(back_scores, key_rows, "hqk,khd->qhd")
    back_keys = contract(back_scores, queries, "hqk,qhd->khd")
    back_mixed = jnp.concatenate(
        [
            back_queries.reshape(row_count, features),
            back_keys.reshape(row_count, features),
            back_values.reshape(row_count, features),
        ],
        axis=1,
    ).astype(jnp.bfloat16)
    grad_qkv = contract(normed, back_mixed, "pc,pe->ce")
    back_normed = contract(back_mixed, w_qkv, "pe,ce->pc")
    back_inputs, grad_gain_attn = norm_attn_back(back_normed)
    back_block = (back_after + back_inputs).astype(jnp.bfloat16)
    gradients = (grad_gain_attn, grad_gain_mlp, grad_qkv, grad_out, grad_up, grad_down, grad_dec)
    return (decoded.astype(jnp.bfloat16), back_block, gradients, mask_term)


def per_device(
    tokens,
    gain_attn,
    gain_mlp,
    w_qkv,
    w_out,
    w_up,
    w_down,
    w_dec,
    mask_token,
    clip_lengths,
    vis_index,
    pos_index,
    cotangent,
):
    shards = (gain_attn, gain_mlp, w_qkv, w_out, w_up, w_down, w_dec)
    spread = lax.axis_size(("dp", "fsdp"))
    running = tuple(
        (jnp.zeros((piece.shape[0] * spread,) + piece.shape[1:], jnp.float32) for piece in shards)
    )
    devices = lax.axis_size("dp")
    device = lax.axis_index("dp")
    micro_count = tokens.shape[1]
    row_count = tokens.shape[2]
    features = tokens.shape[3]
    slot_count = -(-row_count // devices)
    mask_sum = jnp.zeros(mask_token.shape, jnp.float32)
    decoded_all = []
    returned_all = []
    for micro_step in range(micro_count):
        params = (
            lax.all_gather(shards[0], ("dp", "fsdp"), axis=0, tiled=True),
            lax.all_gather(shards[1], ("dp", "fsdp"), axis=0, tiled=True),
            lax.all_gather(shards[2], ("dp", "fsdp"), axis=0, tiled=True),
            lax.all_gather(shards[3], ("dp", "fsdp"), axis=0, tiled=True),
            lax.all_gather(shards[4], ("dp", "fsdp"), axis=0, tiled=True),
            lax.all_gather(shards[5], ("dp", "fsdp"), axis=0, tiled=True),
            lax.all_gather(shards[6], ("dp", "fsdp"), axis=0, tiled=True),
        )
        lengths = clip_lengths[0, micro_step].reshape(devices, -1)
        filled = jnp.sum(lengths, axis=1)
        offsets = jnp.cumsum(filled) - filled
        leading = (device - offsets) % devices
        first_row = (offsets + leading) // devices
        slot_index = jnp.arange(slot_count)
        sent_live = leading[None, :] + slot_index[:, None] * devices < filled[None, :]
        pick_rows = jnp.where(sent_live, first_row[None, :] + slot_index[:, None], row_count)
        source_rows = jnp.concatenate(
            [tokens[0, micro_step], jnp.zeros((1, features), tokens.dtype)], axis=0
        )
        outgoing = jnp.take(source_rows, pick_rows, axis=0)
        incoming = lax.all_to_all(outgoing, "dp", split_axis=1, concat_axis=1, tiled=True)
        own_offset = lax.dynamic_index_in_dim(offsets, device, 0, keepdims=False)
        block_in = jnp.roll(incoming, -own_offset, axis=1).reshape(slot_count * devices, features)[
            :row_count
        ]
        own_lengths = lax.dynamic_index_in_dim(lengths, device, 0, keepdims=False)
        decoded, back_block, gradients, mask_term = layer_pass(
            block_in,
            own_lengths,
            vis_index[0, micro_step],
            pos_index[0, micro_step],
            cotangent[0, micro_step],
            params,
            mask_token,
        )
        running = tuple(
            (total_piece + new_piece for total_piece, new_piece in zip(running, gradients))
        )
        mask_sum = mask_sum + mask_term
        padded_back = jnp.concatenate(
            [back_block, jnp.zeros((slot_count * devices - row_count, features), jnp.bfloat16)],
            axis=0,
        )
        outgoing_back = jnp.roll(
            padded_back.reshape(slot_count, devices, features), own_offset, axis=1
        )
        incoming_back = lax.all_to_all(outgoing_back, "dp", split_axis=1, concat_axis=1, tiled=True)
        returned = (
            jnp.zeros((row_count + 1, features), jnp.bfloat16)
            .at[pick_rows]
            .add(incoming_back)[:row_count]
        )
        decoded_all.append(decoded)
        returned_all.append(returned)
    shares = (
        lax.psum_scatter(running[0], ("dp", "fsdp"), scatter_dimension=0, tiled=True),
        lax.psum_scatter(running[1], ("dp", "fsdp"), scatter_dimension=0, tiled=True),
        lax.psum_scatter(running[2], ("dp", "fsdp"), scatter_dimension=0, tiled=True),
        lax.psum_scatter(running[3], ("dp", "fsdp"), scatter_dimension=0, tiled=True),
        lax.psum_scatter(running[4], ("dp", "fsdp"), scatter_dimension=0, tiled=True),
        lax.psum_scatter(running[5], ("dp", "fsdp"), scatter_dimension=0, tiled=True),
        lax.psum_scatter(running[6], ("dp", "fsdp"), scatter_dimension=0, tiled=True),
    )
    mask_grad = lax.psum(mask_sum, ("dp", "fsdp"))
    return (
        jnp.stack(decoded_all)[None],
        jnp.stack(returned_all)[None],
        shares[0],
        shares[1],
        shares[2],
        shares[3],
        shares[4],
        shares[5],
        shares[6],
        mask_grad,
    )


BF = jnp.bfloat16
F32 = jnp.float32
MESH = pl.DeviceIdType.MESH
MICROS = 2
RP = 320
RT = MICROS * RP
D = 768
DD = 384
FULL = 3136
NZ, NY, NX = 4, 2, 2
CHIPS = NZ * NY * NX
CH = 48
PK = 1024
C_QKV = (0, 640, 1024)
C_DEC, C_OUT, C_UP, C_DOWN, C_ALL = 384, 1408, 1792, 3328, 4864
SWAPPED = C_DOWN
GATHERS = (
    (0, 384, 640, False),
    (640, 128, 384, False),
    (1024, 256, 384, False),
    (C_OUT, 128, 384, False),
    (C_UP, 384, 768, False),
    (C_UP + 768, 384, 768, False),
    (C_DOWN, 384, 768, False),
    (C_DOWN + 768, 256, 384, False),
    (C_DOWN + 1152, 128, 384, True),
)
SUMS = (
    (True, 0, 256, 384, True),
    (True, 384, 128, 384, False),
    (True, 768, 384, 768, False),
    (False, C_DEC, 128, 256, False),
    (False, C_DOWN, 384, 768, False),
    (False, C_DOWN + 768, 384, 768, False),
    (False, C_OUT, 128, 384, False),
    (False, C_UP, 256, 384, False),
    (False, C_UP + 384, 128, 384, False),
    (False, C_UP + 768, 256, 384, False),
)
SUM_AT = (0, 384, 768, 1536, 1792, 2560, 3328, 3712, 4096, 4480)
Z_AT = (0, 3712, 4096, 4480)
SLOTS = 3
YC = 448
EC = 224


(
    S_BEGIN, S_COMPOSE, S_LOAD, S_SEND, S_LAYOUT, S_PROJ, S_BLOCKS, S_GAINS, S_LN1, S_QKV, S_ATT, S_X1, S_UP, S_BDEC,
    S_GDOWN, S_X2, S_Z, S_BDOWN, S_GUP, S_BUP, S_BOUT, S_ATTB, S_BQKV, S_RET, S_GQKV, S_TAB, S_DEC, S_COLL, S_VEC, S_END,
    S_G, S_R,
) = range(32)


def _nn(a, b):
    return lax.dot_general(a, b, (((1,), (0,)), ((), ())), preferred_element_type=F32)


def _nt(a, b):
    return lax.dot_general(a, b, (((1,), (1,)), ((), ())), preferred_element_type=F32)


def _tn(a, b):
    return lax.dot_general(a, b, (((0,), (0,)), ((), ())), preferred_element_type=F32)


def _iota(shape, dim):
    return lax.broadcasted_iota(jnp.int32, shape, dim)


def _mega(
    tok, i0, i1, i2, i3, i4, i5, i6, i7, i8, i9, i10, cot,
    o_rows, o_tok, e0, e1, e2, e3, e4, e5,
    w_qkv, w_out, w_up, w_dec, w_down, gain_a, gain_m, mask_tok, lens, vis, pos,
    o_qkv, o_out, o_up, o_dec, o_down, o_vec,
    W, gD, big, X, A, Tb, Q, O, X1, H, G, GP, X2, dZ, dX, dW, Zx, outg, inc, bias,
    tokb, r0, r1a, r1b, r2a, r2b, r3, r4, fin, decg, posr, vec, rv,
    ik, ek, yk, tk, ok, swk, agz, ag1, ag2, ag3, a2, a2b, rs0, rs1, rs2, rs3, rs4, rvk, rsz,
):
    dp = lax.axis_index("dp")
    f = lax.axis_index("fsdp")
    x = lax.rem(dp, 2)
    y = lax.rem(lax.div(dp, 2), 2)
    z = lax.div(dp, 4)
    sib = (dp, 1 - f)
    xn = (dp + 1 - 2 * x, f)
    yn = (dp + 2 - 4 * y, f)
    E = {}

    def zpeer(k):
        return lax.rem(z + k, NZ)

    def dev_z(k):
        return (lax.rem(dp + 4 * k, CHIPS), f)

    def peer(k):
        return (lax.rem(dp + k, CHIPS), f)

    def remote(src, dst, sems, idx, dev):
        c = pltpu.make_async_remote_copy(
            src_ref=src, dst_ref=dst, send_sem=sems.at[(0,) + idx], recv_sem=sems.at[(1,) + idx],
            device_id=dev, device_id_type=MESH,
        )
        c.start()
        return c

    def wait(copies):
        for c in copies:
            c.wait()

    flight = {}

    def gather(p, step):
        c0, a, n, late = GATHERS[p]
        ca, cb, cn = slice(c0, c0 + a), slice(c0 + a, c0 + n), slice(c0, c0 + n)
        if step > 0:
            wait(flight["g", p])
        zs = z if late else slice(None)
        if step == (2 if late else 0):
            part = W.at[f, z, :, :, :, cn] if late else W.at[f, z, y, x, :, cn]
            cps = [remote(part, part, agz, (p, k - 1), dev_z(k)) for k in range(1, NZ)]
        elif step == (0 if late else 1):
            pa, pb = W.at[f, zs, y, x, :, ca], W.at[f, zs, y, x, :, cb]
            cps = [remote(pa, pa, ag1, (p, 0), yn), remote(pb, pb, ag1, (p, 1), xn)]
        elif step == (1 if late else 2):
            pa, pb = W.at[f, zs, :, x, :, ca], W.at[f, zs, y, :, :, cb]
            cps = [remote(pa, pa, ag2, (p, 0), xn), remote(pb, pb, ag2, (p, 1), yn)]
        elif step == 3:
            part = W.at[f, :, :, :, :, cn]
            cps = [remote(part, part, ag3, (p,), sib)]
        else:
            cps = []
        flight["g", p] = cps

    def place(p, h, val):
        if p < 3:
            rows_at, cols_at = ((0, 0), (0, 384), (48, 0))[p]
            o_down[rows_at : rows_at + 48, cols_at : cols_at + val.shape[1]] = val
        elif p == 3:
            decg[:, pl.ds(pl.multiple_of(256 * h, 128), 256)] = val
        elif p < 6:
            o_up[:, pl.ds(pl.multiple_of(1536 * h + 768 * (p - 4), 128), 768)] = val
        elif p == 6:
            o_out[:, pl.ds(pl.multiple_of(384 * h, 128), 384)] = val
        else:
            for i in range(3):
                at = pl.multiple_of(768 * i + 128 * (p - 7 + 3 * h), 128)
                o_qkv[:, pl.ds(at, 128)] = val[:, 128 * i : 128 * i + 128]

    def reduce(p, step):
        own, c0, a, w, early = SUMS[p]
        ref = gD if own else W
        b = w - a
        ca, cb, cw = slice(c0, c0 + a), slice(c0 + a, c0 + w), slice(c0, c0 + w)
        sl = p % SLOTS
        at = SUM_AT[p]
        if step > 0:
            wait(flight["r", p])
        cps = []

        def send_first(zs, to):
            return [
                remote(ref.at[f, zs, :, 1 - x, :, ca], r1a.at[sl, to, :, :, 0:a], rs1, (p, 0), xn),
                remote(ref.at[f, zs, 1 - y, :, :, cb], r1b.at[sl, to, :, :, 0:b], rs1, (p, 1), yn),
            ]

        def send_second(zs, to):
            return [
                remote(ref.at[f, zs, 1 - y, x, :, ca], r2a.at[sl, to, :, 0:a], rs2, (p, 0), yn),
                remote(ref.at[f, zs, y, 1 - x, :, cb], r2b.at[sl, to, :, 0:b], rs2, (p, 1), xn),
            ]

        def add_first(i, to):
            ref[f, i, :, x, :, ca] = ref[f, i, :, x, :, ca] + r1a[sl, to, :, :, 0:a]
            ref[f, i, y, :, :, cb] = ref[f, i, y, :, :, cb] + r1b[sl, to, :, :, 0:b]

        def add_second(i, to):
            ref[f, i, y, x, :, ca] = ref[f, i, y, x, :, ca] + r2a[sl, to, :, 0:a]
            ref[f, i, y, x, :, cb] = ref[f, i, y, x, :, cb] + r2b[sl, to, :, 0:b]

        def over_z(add):
            def body(i, carry):
                add(i, i)
                return carry

            lax.fori_loop(0, NZ, body, 0)

        if step == 0:
            cps = [remote(ref.at[1 - f, :, :, :, :, cw], r0.at[p % 2, :, :, :, :, 0:w], rs0, (p,), sib)]
        elif step == 1:

            def add(i, carry):
                ref[f, i, :, :, :, cw] = ref[f, i, :, :, :, cw] + r0[p % 2, i, :, :, :, 0:w]
                return carry

            lax.fori_loop(0, NZ, add, 0)
            if early:
                for k in range(1, NZ):
                    for c in range(4):
                        src = ref.at[f, zpeer(k), c // 2, c % 2, :, cw]
                        cps.append(remote(src, r3.at[k - 1, :, Z_AT[c] : Z_AT[c] + w], rsz, (k - 1, c), dev_z(k)))
            else:
                cps = send_first(slice(None), slice(None))
        elif step == 2:
            if early:
                for c in range(4):
                    total = ref[f, z, c // 2, c % 2, :, cw].astype(F32)
                    for k in range(NZ - 1):
                        total = total + r3[k, :, Z_AT[c] : Z_AT[c] + w].astype(F32)
                    ref[f, z, c // 2, c % 2, :, cw] = total.astype(BF)
                cps = send_first(z, 0)
            else:
                over_z(add_first)
                cps = send_second(slice(None), slice(None))
        elif step == 3:
            if early:
                add_first(z, 0)
                cps = send_second(z, 0)
            else:
                over_z(add_second)
                for k in range(1, NZ):
                    src = ref.at[f, zpeer(k), y, x, :, cw]
                    cps.append(remote(src, r3.at[k - 1, :, at : at + w], rs3, (p, k - 1), dev_z(k)))
        elif step == 4:
            total = ref[f, z, y, x, :, cw].astype(F32)
            if early:
                total = total + jnp.concatenate([r2a[sl, 0, :, 0:a], r2b[sl, 0, :, 0:b]], axis=1).astype(F32)
            else:
                for k in range(NZ - 1):
                    total = total + r3[k, :, at : at + w].astype(F32)
            if own:
                place(p, None, total)
            else:
                fin[p % 2, :, 0:w] = total
                place(p, f, fin[p % 2, pl.ds(pl.multiple_of(24 * f, 8), 24), 0:w])
                src = fin.at[p % 2, pl.ds(pl.multiple_of(24 * (1 - f), 8), 24), 0:w]
                cps = [remote(src, r4.at[:, at - 1536 : at - 1536 + w], rs4, (p,), sib)]
        else:
            if not own:
                place(p, 1 - f, r4[:, at - 1536 : at - 1536 + w])
            finished(p)
        flight["r", p] = cps

    def scalars():
        E["filled"] = [[None] * CHIPS for _ in range(MICROS)]
        E["before"] = [[None] * CHIPS for _ in range(MICROS)]
        E["mine"], E["own"] = [], []
        for m in range(MICROS):
            running = jnp.int32(0)
            at_me = jnp.int32(0)
            for d in range(CHIPS):
                total = lens[m, 4 * d] + lens[m, 4 * d + 1] + lens[m, 4 * d + 2] + lens[m, 4 * d + 3]
                E["filled"][m][d] = total
                E["before"][m][d] = running
                at_me = at_me + jnp.where(dp == d, running, 0)
                running = running + total
            run, frun = jnp.int32(0), jnp.int32(0)
            ends, starts = [], []
            for c in range(4):
                n = lens[m, 4 * dp + c]
                run = run + n
                ends.append(run)
                starts.append(frun)
                for k in range(1, 5):
                    frun = frun + jnp.where(n >= 78 * k, 784, 0)
            E["mine"].append((at_me, run))
            E["own"].append((ends, starts, frun))

    def pick(m, d):
        lead = (dp - E["before"][m][d]) & (CHIPS - 1)
        first = (E["before"][m][d] + lead) >> 4
        return first, (E["filled"][m][d] - lead + CHIPS - 1) >> 4

    def pack(src, params):
        lane = _iota((16, RP), 1)
        sub = _iota((16, RP), 0)
        late = 16 + (sub & 3)
        for d in range(CHIPS):
            base, step, limit = params(d)
            want = base + step * sub
            O[16 * d : 16 * d + 16, 0:RP] = jnp.where((lane == want) & (want < limit), 1.0, 0.0).astype(BF)
            want = base + step * late
            O[256 + 16 * d : 272 + 16 * d, 0:RP] = jnp.where((lane == want) & (want < limit), 1.0, 0.0).astype(BF)
        head = _nn(O[0:256, 0:RP], src).astype(BF)
        third = (_iota((256, RP), 0) & 15) >> 2
        late_rows = O[256:512, 0:RP]
        rest = None
        for s in range(3):
            part = _nn(jnp.where(third == s, late_rows, jnp.zeros((), BF)), src[:, 256 * s : 256 * s + 256])
            rest = part if rest is None else rest + part
        return head, rest.astype(BF)

    def send_rows(m, src, params, sems):
        head, rest = pack(src, params)
        outg[m, :, :, 0:D] = head.reshape(CHIPS, 16, D)
        outg[m, :, :, D:PK] = rest.reshape(CHIPS, 16, PK - D)
        cps = []
        for k in range(1, CHIPS):
            to = peer(k)
            cps.append(remote(outg.at[m, to[0]], inc.at[m, dp], sems, (m, k - 1), to))
        inc[m, dp] = outg[m, dp]
        flight["a", m] = cps

    def rows(m):
        return slice(m * RP, (m + 1) * RP)

    def wt(h, c0, n):
        return W[h, :, :, :, :, c0 : c0 + n].reshape(D, n)

    def both(c0, n):
        return jnp.concatenate([wt(0, c0, n), wt(1, c0, n)], axis=1)

    def down_rows(q):
        return jnp.concatenate(
            [W[h, q, i // 2, i % 2, :, C_DOWN + 768 * k : C_DOWN + 768 * k + 768] for i in range(4) for h in range(2) for k in range(2)],
            axis=0,
        )

    def ln_parts(v):
        center = v - jnp.mean(v, axis=-1, keepdims=True)
        r = lax.rsqrt(jnp.mean(center * center, axis=-1, keepdims=True) + EPS)
        return center * r, r

    def ln_back(dh, xhat, r, gain):
        dxh = dh * gain
        return r * (dxh - jnp.mean(dxh, axis=-1, keepdims=True) - xhat * jnp.mean(dxh * xhat, axis=-1, keepdims=True))

    sub_p = _iota((RP, 1), 0)
    lane_p = _iota((1, RP), 1)

    sources = (i0, i1, i2, i3, i4, i5, i6, i7, i8, i9, i10)
    held = (w_qkv, w_out, w_up, w_dec, w_down, gain_a, gain_m, mask_tok, lens, vis, pos)
    made = {0: (o_qkv, e0), 1: (o_out, e1), 2: (o_up, e2), 3: (o_dec, e3), 4: (o_down, e4), 5: (o_vec, e5)}
    pending = {0: {7, 8, 9}, 1: {6}, 2: {4, 5}, 3: {3}, 4: {0, 1, 2}}

    def emit(i):
        flight["e", i] = [pltpu.make_async_copy(*made[i], ek.at[i])]
        flight["e", i][0].start()

    def finished(p):
        for i, left in pending.items():
            if p in left:
                left.discard(p)
                if not left:
                    if i == 3:
                        o_dec[...] = decg[:, 0:DD]
                    emit(i)

    def begin():
        first = [pltpu.make_async_copy(a, b, ik.at[i]) for i, (a, b) in enumerate(zip(sources, held))]
        for c in first:
            c.start()
        bar = pltpu.get_barrier_semaphore()
        pl.semaphore_signal(bar, inc=1, device_id=sib, device_id_type=MESH)
        for k in range(1, CHIPS):
            pl.semaphore_signal(bar, inc=1, device_id=peer(k), device_id_type=MESH)
        E["tok"] = pltpu.make_async_copy(tok, tokb, tk.at[0])
        E["tok"].start()
        E["y"] = [pltpu.make_async_copy(cot.at[m], big.at[m * FULL : (m + 1) * FULL], yk.at[m]) for m in range(MICROS)]
        for c in E["y"]:
            c.start()
        wait(first)
        n = gain_a.shape[0]
        diag = _iota((n, n), 0) == _iota((n, n), 1)
        lane = _iota((n, 128), 1)

        def column(ref):
            return jnp.sum(jnp.where(diag, jnp.broadcast_to(ref[...].astype(F32)[None, :], (n, n)), 0.0), axis=1, keepdims=True)

        gains = jnp.where(lane == 0, column(gain_a), jnp.where(lane == 1, column(gain_m), 0.0)).astype(BF)
        for h in range(2):
            for p in range(3):
                for i in range(3):
                    j = p + 3 * h
                    c = C_QKV[p] + 128 * i
                    r3[h, 0:24, c : c + 128] = w_qkv[:, 768 * i + 128 * j : 768 * i + 128 * j + 128]
            r3[h, 0:24, C_OUT : C_OUT + 384] = w_out[:, 384 * h : 384 * h + 384]
            r3[h, 0:24, C_UP : C_UP + 1536] = w_up[:, 1536 * h : 1536 * h + 1536]
        r3[0, 0:24, C_DEC : C_DEC + 256] = w_dec[:, 0:256]
        r3[1, 0:24, C_DEC : C_DEC + 128] = w_dec[:, 256:384]
        r3[1, 0:24, C_DEC + 128 : C_DEC + 256] = gains
        W[f, z, y, x, :, C_DOWN : C_DOWN + 768] = w_down[0:CH, :]
        W[f, z, y, x, :, C_DOWN + 768 : C_ALL] = w_down[CH : 2 * CH, :]
        pl.semaphore_wait(bar, CHIPS)
        E["swap"] = remote(r3.at[1 - f, 0:32, 0:SWAPPED], r3.at[2, 0:32, 0:SWAPPED], swk, (0,), sib)
        scalars()

    def compose():
        E["swap"].wait()
        mine_rows = r3[f, 0:24, 0:SWAPPED].astype(F32)
        other_rows = r3[2, 0:24, 0:SWAPPED].astype(F32)
        lower = jnp.where(f == 0, mine_rows, other_rows)
        upper = jnp.where(f == 0, other_rows, mine_rows)
        W[f, z, y, x, :, 0:SWAPPED] = jnp.concatenate([lower, upper], axis=0).astype(BF)

    def load_tokens():
        E["tok"].wait()
        n = tokb.shape[0]
        for m in range(MICROS):
            A[m * RP + 304 : m * RP + 320, :] = jnp.zeros((16, D), BF)
            A[m * RP : m * RP + n, :] = tokb[:, m, :]

    def send_tokens(m):
        def params(d):
            first, count = pick(m, d)
            return first, 1, first + count

        send_rows(m, A[rows(m), :], params, a2)

    def layout():
        n = vis.shape[1]
        diag = _iota((RP, RP), 0) == _iota((RP, RP), 1)
        E["row"], E["col"] = [], []
        for m in range(MICROS):
            ends, starts, _ = E["own"][m]
            v = jnp.concatenate([vis[m : m + 1, :], jnp.zeros((1, RP - n), jnp.int32)], axis=1)

            def clip_of(p):
                return sum((jnp.where(p >= e, 1, 0) for e in ends))

            def start_of(cid):
                return sum((jnp.where(cid == c, starts[c], 0) for c in range(4)))

            cr, cc = clip_of(lane_p), clip_of(sub_p)
            bias[m] = jnp.where(cc == cr, 0.0, NEG).astype(BF)
            E["row"].append(jnp.where(cr < 4, start_of(cr) + v, -1))
            vcol = jnp.sum(jnp.where(diag, jnp.broadcast_to(v.astype(F32), (RP, RP)), 0.0), axis=1, keepdims=True)
            E["col"].append(jnp.where(cc < 4, start_of(cc) + vcol.astype(jnp.int32), -1))
            for c in range(FULL // EC):
                posr[m, c : c + 1, :] = pos[m : m + 1, c * EC : (c + 1) * EC]

    def project_back(m):
        E["y"][m].wait()
        full_total = E["own"][m][2]
        extra = sub_p == RP - 1
        target = E["col"][m]

        def chunk(c, acc):
            spot = _iota((RP, YC), 1) + c * YC
            hit = (spot == target) | (extra & (spot < full_total))
            ys = big[pl.ds(pl.multiple_of(m * FULL + c * YC, 64), YC), :]
            return acc + _nn(jnp.where(hit, 1.0, 0.0).astype(BF), ys)

        acc = lax.fori_loop(0, FULL // YC, chunk, jnp.zeros((RP, DD), F32))
        whole = jnp.sum(jnp.where(extra, acc, 0.0), axis=0, keepdims=True)
        acc = jnp.where(extra, 0.0, acc)
        dZ[rows(m), :] = acc.astype(BF)
        s = whole - jnp.sum(acc, axis=0, keepdims=True)
        E["mask"] = s if m == 0 else E["mask"] + s

    def blocks(m):
        wait(flight["a", m])
        off, count = E["mine"][m]

        def source(p):
            return jnp.where(p < count, ((off + p) & (CHIPS - 1)) * 16, -4096)

        p = sub_p[0:256]
        hit = jnp.where(_iota((256, 256), 1) == source(p) + (p >> 4), 1.0, 0.0).astype(BF)
        got = inc[m].reshape(256, PK)
        X[m * RP : m * RP + 256, :] = _nn(hit, got[:, 0:D]).astype(BF)
        p = sub_p[0:64] + 256
        for s in range(3):
            hit = jnp.where(_iota((64, 256), 1) == source(p) + 4 * s + (p >> 4) - 16, 1.0, 0.0).astype(BF)
            X[m * RP + 256 : m * RP + RP, 256 * s : 256 * s + 256] = _nn(hit, got[:, D:PK]).astype(BF)

    def gains():
        g = jnp.transpose(wt(1, C_DEC + 128, 128).astype(F32))
        E["gain_attn"], E["gain_mlp"] = g[0:1, :], g[1:2, :]
        E["gsum_attn"] = E["gsum_mlp"] = None

    def ln1(m):
        xhat, _ = ln_parts(X[rows(m), :].astype(F32))
        A[rows(m), :] = (xhat * E["gain_attn"]).astype(BF)

    def qkv(p, m):
        res = _nn(A[rows(m), :], both(C_QKV[p], 384)).astype(BF)
        Q[rows(m), 384 * p : 384 * p + 384] = res[:, 0:384]
        Q[rows(m), 384 * p + 1152 : 384 * p + 1536] = res[:, 384:768]

    lane128 = _iota((1, 128), 1)
    head_mask = (lane128 < 64, lane128 >= 64)
    QB = ((0, 128), (128, 128), (256, 64))

    def attend(p, m):
        r = rows(m)

        def pair(i, carry):
            j = p + 3 * i
            at = pl.multiple_of(j * 384, 128)
            q2, k2, v2 = (Q[r, pl.ds(pl.multiple_of(at + 128 * k, 128), 128)] for k in range(3))
            v_t = jnp.transpose(v2)
            for b0, bn in QB:
                halves = []
                for h in range(2):
                    qm = jnp.where(head_mask[h], q2[b0 : b0 + bn], jnp.zeros((), BF))
                    s = _nt(k2, qm) * 0.125 + bias[m, :, b0 : b0 + bn].astype(F32)
                    e = jnp.exp(s - jnp.max(s, axis=0, keepdims=True))
                    pb = (e * (1.0 / jnp.sum(e, axis=0, keepdims=True))).astype(BF)
                    big[pl.ds(pl.multiple_of((m * 12 + 2 * j + h) * RP, 64), RP), b0 : b0 + bn] = pb
                    halves.append(_nn(v_t[64 * h : 64 * h + 64], pb))
                O[m * RP + b0 : m * RP + b0 + bn, pl.ds(pl.multiple_of(j * 128, 128), 128)] = jnp.transpose(jnp.concatenate(halves, axis=0)).astype(BF)
            return carry

        lax.fori_loop(0, 2, pair, 0)

    def attend_back(p, m):
        r = rows(m)

        def pair(i, carry):
            j = p + 3 * i
            at = pl.multiple_of(j * 384, 128)
            cq, ck, cv = (pl.ds(pl.multiple_of(at + 128 * k, 128), 128) for k in range(3))
            q2, k2, v2 = Q[r, cq], Q[r, ck], Q[r, cv]
            do2 = X2[r, pl.ds(pl.multiple_of(j * 128, 128), 128)]
            k_t = jnp.transpose(k2)
            dk = jnp.zeros((RP, 128), F32)
            dv = jnp.zeros((RP, 128), F32)
            for b0, bn in QB:
                halves = []
                for h in range(2):
                    dom = jnp.where(head_mask[h], do2[b0 : b0 + bn], jnp.zeros((), BF))
                    qm = jnp.where(head_mask[h], q2[b0 : b0 + bn], jnp.zeros((), BF))
                    dp_t = _nt(v2, dom)
                    pb = big[pl.ds(pl.multiple_of((m * 12 + 2 * j + h) * RP, 64), RP), b0 : b0 + bn]
                    pf = pb.astype(F32)
                    w = pf * dp_t
                    ds = (w - pf * jnp.sum(w, axis=0, keepdims=True)).astype(BF)
                    halves.append(_nn(k_t[64 * h : 64 * h + 64], ds))
                    dv = dv + _nn(pb, dom)
                    dk = dk + _nn(ds, qm)
                dq = jnp.transpose(jnp.concatenate(halves, axis=0)) * 0.125
                Q[m * RP + b0 : m * RP + b0 + bn, cq] = dq.astype(BF)
            Q[r, ck] = (dk * 0.125).astype(BF)
            Q[r, cv] = dv.astype(BF)
            return carry

        lax.fori_loop(0, 2, pair, 0)

    def after_attention(m):
        x1 = X[rows(m), :].astype(F32) + _nn(O[rows(m), :], both(C_OUT, 384))
        X1[rows(m), :] = x1
        xhat, _ = ln_parts(x1)
        H[rows(m), :] = (xhat * E["gain_mlp"]).astype(BF)

    def up(b, h):
        w = wt(h, C_UP + 768 * b, 768)
        c0 = 1536 * h + 768 * b

        def body(m, carry):
            at = pl.ds(pl.multiple_of(m * RP, RP), RP)
            u = _nn(H[at, :], w)
            cdf = 0.5 * (1.0 + lax.erf(u * (1.0 / math.sqrt(2.0))))
            pdf = jnp.exp(u * u * -0.5) * (1.0 / math.sqrt(2.0 * math.pi))
            G[at, c0 : c0 + 768] = (u * cdf).astype(BF)
            GP[at, c0 : c0 + 768] = (cdf + u * pdf).astype(BF)
            return carry

        lax.fori_loop(0, MICROS, body, 0)

    def dec_weights():
        return jnp.concatenate([wt(0, C_DEC, 256), wt(1, C_DEC, 128)], axis=1)

    def back_dec():
        w = dec_weights()
        for m in range(MICROS):
            d = _nt(dZ[rows(m), :], w)
            dX[rows(m), :] = d
            dW[rows(m), :] = d.astype(BF)

    def put_grad(ref, h, c0, n, val):
        ref[h, :, :, :, :, c0 : c0 + n] = val.astype(BF).reshape(NZ, NY, NX, CH, n)

    def grad_down(q):
        val = _tn(G[:, 768 * q : 768 * q + 768], dW[...]).astype(BF)
        for i in range(4):
            for h in range(2):
                for k in range(2):
                    n = 4 * i + 2 * h + k
                    gD[h, q, i // 2, i % 2, :, 768 * k : 768 * k + 768] = val[48 * n : 48 * n + 48, :]

    def after_mlp(m):
        acc = X1[rows(m), :]
        for q in range(4):
            acc = acc + _nn(G[rows(m), 768 * q : 768 * q + 768], down_rows(q))
        X2[rows(m), :] = acc.astype(BF)

    def project():
        w = dec_weights()
        for m in range(MICROS):
            Zx[rows(m), :] = _nn(X2[rows(m), :], w).astype(BF)
        gd = _tn(X2[...], dZ[...])
        put_grad(W, 0, C_DEC, 256, gd[:, 0:256])
        put_grad(W, 1, C_DEC, 128, gd[:, 256:384])

    def back_down(q):
        w = down_rows(q)
        for m in range(MICROS):
            back = _nt(dW[rows(m), :], w)
            at = slice(768 * q, 768 * q + 768)
            GP[rows(m), at] = (back * GP[rows(m), at].astype(F32)).astype(BF)

    def grad_up(b):
        if b == 0:
            Tb[...] = jnp.transpose(H[...])
        for h in range(2):
            c0 = 1536 * h + 768 * b
            put_grad(W, h, C_DOWN + 768 * b, 768, _nn(Tb[...], GP[:, c0 : c0 + 768]))

    def back_up(m):
        dh = _nt(GP[rows(m), 0:1536], wt(0, C_UP, 1536)) + _nt(GP[rows(m), 1536:3072], wt(1, C_UP, 1536))
        xhat, r = ln_parts(X1[rows(m), :])
        s = jnp.sum(dh * xhat, axis=0, keepdims=True)
        E["gsum_mlp"] = s if m == 0 else E["gsum_mlp"] + s
        dx1 = dX[rows(m), :] + ln_back(dh, xhat, r, E["gain_mlp"])
        dX[rows(m), :] = dx1
        dW[rows(m), :] = dx1.astype(BF)

    def back_out():
        w = both(C_OUT, 384)
        for m in range(MICROS):
            X2[rows(m), :] = _nt(dW[rows(m), :], w).astype(BF)
        go = _tn(O[...], dW[...])
        put_grad(W, 0, C_OUT, 384, go[:, 0:384])
        put_grad(W, 1, C_OUT, 384, go[:, 384:768])

    def back_qkv(m):
        da = None
        for h in range(2):
            w = jnp.concatenate([wt(h, C_QKV[p], 384) for p in range(3)], axis=1)
            part = _nt(Q[rows(m), 1152 * h : 1152 * h + 1152], w)
            da = part if da is None else da + part
        xhat, r = ln_parts(X[rows(m), :].astype(F32))
        s = jnp.sum(da * xhat, axis=0, keepdims=True)
        E["gsum_attn"] = s if m == 0 else E["gsum_attn"] + s
        H[rows(m), :] = (dX[rows(m), :] + ln_back(da, xhat, r, E["gain_attn"])).astype(BF)

    def return_rows(m):
        off, count = E["mine"][m]

        def params(d):
            return (d - off) & (CHIPS - 1), CHIPS, count

        send_rows(m, H[rows(m), :], params, a2b)

    def grad_qkv(p):
        if p == 0:
            X2_t = jnp.transpose(A[...])
            Tb[...] = X2_t
        val = _nn(Tb[...], jnp.concatenate([Q[:, 384 * p : 384 * p + 384], Q[:, 384 * p + 1152 : 384 * p + 1536]], axis=1))
        put_grad(W, 0, C_UP + 384 * p, 384, val[:, 0:384])
        put_grad(W, 1, C_UP + 384 * p, 384, val[:, 384:768])

    def tables():
        chan = _iota((64, DD), 1)
        even = (chan & 1) == 0
        rate = jnp.exp((chan - (chan & 1)).astype(F32) * (-math.log(10000.0) / DD))
        ang = (32 * _iota((64, DD), 0)).astype(F32) * rate
        sa, ca = jnp.sin(ang), jnp.cos(ang)
        angb = _iota((64, DD), 0).astype(F32) * rate
        sb, cb = jnp.sin(angb), jnp.cos(angb)
        GP[0:256, 0 : 4 * DD] = jnp.zeros((256, 4 * DD), BF)

        def put(at, col, val):
            hi = val.astype(BF)
            GP[at : at + 64, col : col + DD] = hi
            GP[128 + at : 192 + at, col : col + DD] = (val - hi.astype(F32)).astype(BF)

        put(0, 0, jnp.where(even, sa, ca))
        put(0, DD, jnp.where(even, ca, -sa))
        put(64, 2 * DD, cb)
        put(64, 3 * DD, sb)

    def decode(m, lo, hi):
        full_total = E["own"][m][2]
        target = E["row"][m]
        mt = mask_tok[...].astype(F32)[None, :]

        def chunk(c, carry):
            spot = _iota((EC, RP), 0) + c * EC
            hit = jnp.where(spot == target, 1.0, 0.0).astype(BF)
            mz = _nn(hit, jnp.concatenate([Zx[rows(m), :], jnp.ones((RP, 128), BF)], axis=1))
            ps = posr[m, pl.ds(c, 1), :]
            kk = _iota((256, EC), 0) & 127
            want = jnp.where(kk < 64, ps >> 5, (ps & 31) + 64)
            code = _tn(jnp.where(kk == want, 1.0, 0.0).astype(BF), GP[0:256, 0 : 4 * DD])
            pe = code[:, 0:DD] * code[:, 2 * DD : 3 * DD] + code[:, DD : 2 * DD] * code[:, 3 * DD : 4 * DD]
            live = jnp.where(_iota((EC, 1), 0) + c * EC < full_total, 1.0, 0.0)
            cov = jnp.concatenate([mz[:, DD:512]] * 3, axis=1)
            val = mz[:, 0:DD] + (live - cov) * mt + live * pe
            big[pl.ds(pl.multiple_of(m * FULL + c * EC, 32), EC), :] = val.astype(BF)
            return carry

        lax.fori_loop(lo, hi, chunk, 0)
        if hi == FULL // EC:
            c = pltpu.make_async_copy(big.at[m * FULL : (m + 1) * FULL], o_rows.at[m], ok.at[m])
            c.start()
            flight["d", m] = [c]

    def collect(m):
        wait(flight["a", m])
        lane = _iota((1, 256), 1)
        early = jnp.full((1, 256), -1, jnp.int32)
        late = jnp.full((1, 256), -1, jnp.int32)
        for d in range(CHIPS):
            first, count = pick(m, d)
            s = lane - 16 * d
            here = (s >= 0) & (s < 16)
            early = jnp.where(here & (s < count), first + s, early)
            t = 16 + (s & 3)
            late = jnp.where(here & (t < count), first + t, late)
        got = inc[m].reshape(256, PK)
        row = _iota((RP, 256), 0)
        head = _nn(jnp.where(row == early, 1.0, 0.0).astype(BF), got[:, 0:D])
        third = (lane & 15) >> 2
        parts = []
        for s in range(3):
            hit = jnp.where((row == late) & (third == s), 1.0, 0.0).astype(BF)
            parts.append(head[:, 256 * s : 256 * s + 256] + _nn(hit, got[:, D:PK]))
        back = jnp.concatenate(parts, axis=1).astype(BF)
        tokb[:, m, :] = back[0 : tokb.shape[0]]

    def vector(step):
        if step > 0:
            wait(flight["v"])
        if step == 0:
            ga, gm = E["gsum_attn"], E["gsum_mlp"]
            vec[...] = jnp.concatenate(
                [E["mask"], ga[:, 0:DD], ga[:, DD:D], gm[:, 0:DD], gm[:, DD:D], jnp.zeros((3, DD), F32)], axis=0
            )
        elif step < 4:
            vec[...] = vec[...] + rv[step - 1]
        if step < 3:
            flight["v"] = [remote(vec, rv.at[step], rvk, (step,), (sib, xn, yn)[step])]
        elif step == 3:
            flight["v"] = [remote(vec, rv.at[2 + k], rvk, (2 + k,), dev_z(k)) for k in range(1, NZ)]
        else:
            o_vec[...] = vec[...] + rv[3] + rv[4] + rv[5]
            emit(5)

    def end():
        c = pltpu.make_async_copy(tokb, o_tok, tk.at[0])
        c.start()
        c.wait()
        for i in range(6):
            wait(flight["e", i])
        wait(flight["d", 0])
        wait(flight["d", 1])

    steps = {
        S_BEGIN: begin, S_COMPOSE: compose, S_LOAD: load_tokens, S_SEND: send_tokens, S_LAYOUT: layout, S_PROJ: project_back,
        S_BLOCKS: blocks, S_GAINS: gains, S_LN1: ln1, S_QKV: qkv, S_ATT: attend, S_X1: after_attention, S_UP: up, S_BDEC: back_dec,
        S_GDOWN: grad_down, S_X2: after_mlp, S_Z: project, S_BDOWN: back_down, S_GUP: grad_up, S_BUP: back_up, S_BOUT: back_out,
        S_ATTB: attend_back, S_BQKV: back_qkv, S_RET: return_rows, S_GQKV: grad_qkv, S_TAB: tables, S_DEC: decode, S_COLL: collect,
        S_VEC: vector, S_END: end, S_G: gather, S_R: reduce,
    }
    for name, *args in ORDER:
        steps[name](*args)


ORDER = (
    (S_BEGIN,), (S_COMPOSE,), (S_G, 1, 0), (S_G, 8, 0), (S_LAYOUT,), (S_PROJ, 0), (S_G, 0, 0), (S_G, 8, 1), (S_G, 1, 1),
    (S_G, 1, 2), (S_LOAD,), (S_G, 2, 0), (S_G, 3, 0), (S_G, 0, 1), (S_SEND, 0), (S_G, 2, 1), (S_G, 3, 1), (S_G, 0, 2),
    (S_G, 5, 0), (S_G, 1, 3), (S_G, 2, 2), (S_PROJ, 1), (S_G, 3, 2), (S_G, 0, 3), (S_G, 4, 0), (S_G, 5, 1), (S_G, 1, 4),
    (S_G, 2, 3), (S_G, 3, 3), (S_G, 0, 4), (S_GAINS,), (S_SEND, 1), (S_BLOCKS, 0), (S_LN1, 0), (S_QKV, 0, 0), (S_ATT, 0, 0),
    (S_G, 4, 1), (S_BDEC,), (S_G, 2, 4), (S_QKV, 2, 0), (S_ATT, 2, 0), (S_QKV, 1, 0), (S_G, 5, 2), (S_G, 3, 4), (S_ATT, 1, 0),
    (S_X1, 0), (S_G, 7, 0), (S_G, 4, 2), (S_G, 6, 0), (S_BLOCKS, 1), (S_LN1, 1), (S_QKV, 0, 1), (S_QKV, 2, 1), (S_ATT, 2, 1),
    (S_QKV, 1, 1), (S_ATT, 1, 1), (S_G, 5, 3), (S_G, 8, 2), (S_G, 7, 1), (S_ATT, 0, 1), (S_G, 6, 1), (S_X1, 1), (S_G, 4, 3),
    (S_G, 5, 4), (S_UP, 1, 1), (S_G, 7, 2), (S_UP, 1, 0), (S_G, 4, 4), (S_UP, 0, 1), (S_G, 6, 2), (S_UP, 0, 0), (S_GDOWN, 2),
    (S_GDOWN, 3), (S_GDOWN, 1), (S_G, 7, 3), (S_GDOWN, 0), (S_R, 0, 0), (S_G, 7, 4), (S_G, 8, 3), (S_R, 0, 1), (S_R, 1, 0),
    (S_G, 6, 3), (S_R, 1, 1), (S_G, 8, 4), (S_R, 2, 0), (S_G, 6, 4), (S_BDOWN, 3), (S_BDOWN, 2), (S_R, 2, 1), (S_X2, 0),
    (S_BDOWN, 1), (S_R, 1, 2), (S_X2, 1), (S_Z,), (S_BDOWN, 0), (S_R, 3, 0), (S_R, 0, 2), (S_GUP, 0), (S_R, 1, 3),
    (S_R, 0, 3), (S_R, 2, 2), (S_BUP, 0), (S_R, 0, 4), (S_R, 3, 1), (S_R, 4, 0), (S_GUP, 1), (S_R, 2, 3), (S_R, 4, 1),
    (S_BUP, 1), (S_BOUT,), (S_ATTB, 1, 0), (S_R, 4, 2), (S_R, 5, 0), (S_ATTB, 2, 0), (S_R, 5, 1), (S_R, 6, 0), (S_R, 4, 3),
    (S_R, 1, 4), (S_R, 3, 2), (S_ATTB, 0, 0), (S_BQKV, 0), (S_RET, 0), (S_ATTB, 1, 1), (S_R, 5, 2), (S_ATTB, 0, 1),
    (S_R, 2, 4), (S_GQKV, 0), (S_R, 3, 3), (S_R, 6, 1), (S_R, 7, 0), (S_ATTB, 2, 1), (S_R, 7, 1), (S_R, 5, 3), (S_GQKV, 1),
    (S_R, 8, 0), (S_BQKV, 1), (S_VEC, 0), (S_GQKV, 2), (S_R, 8, 1), (S_R, 6, 2), (S_R, 4, 4), (S_RET, 1), (S_R, 7, 2),
    (S_R, 9, 0), (S_TAB,), (S_DEC, 0, 0, 7), (S_VEC, 1), (S_R, 6, 3), (S_R, 9, 1), (S_DEC, 1, 0, 7), (S_R, 8, 2), (S_R, 7, 3),
    (S_DEC, 0, 7, 14), (S_VEC, 2), (S_R, 9, 2), (S_R, 4, 5), (S_R, 6, 4), (S_R, 8, 3), (S_R, 3, 4), (S_R, 1, 5), (S_COLL, 1),
    (S_R, 6, 5), (S_R, 3, 5), (S_R, 5, 4), (S_R, 2, 5), (S_R, 0, 5), (S_COLL, 0), (S_R, 5, 5), (S_R, 7, 4), (S_R, 9, 3),
    (S_VEC, 3), (S_DEC, 1, 7, 14), (S_R, 8, 4), (S_R, 7, 5), (S_R, 9, 4), (S_R, 8, 5), (S_VEC, 4), (S_R, 9, 5), (S_END,),
)


def _mega_call(tok, w_qkv, w_out, w_up, w_dec, w_down, gain_a, gain_m, mask_tok, lens, vis, pos, cot):
    vm = lambda *s: pltpu.VMEM(s[:-1], s[-1])
    sem = lambda *s: pltpu.SemaphoreType.DMA(s)
    ANY = pl.BlockSpec(memory_space=pl.ANY)
    raw = (w_qkv, w_out, w_up, w_dec, w_down, gain_a, gain_m, mask_tok, lens, vis, pos)
    grads = [jax.ShapeDtypeStruct(w.shape, F32) for w in raw[:5]] + [jax.ShapeDtypeStruct((8, DD), F32)]
    held = [(pltpu.SMEM if a is lens else pltpu.VMEM)(a.shape, a.dtype) for a in raw] + [pltpu.VMEM(a.shape, F32) for a in grads]
    scratch = [
        vm(2, NZ, NY, NX, CH, C_ALL, BF),
        vm(2, NZ, NY, NX, CH, 1536, BF),
        vm(24 * RP, DD, BF),
        vm(RT, D, BF),
        vm(RT, D, BF),
        vm(D, RT, BF),
        vm(RT, 3 * D, BF),
        vm(RT, D, BF),
        vm(RT, D, F32),
        vm(RT, D, BF),
        vm(RT, 4 * D, BF),
        vm(RT, 4 * D, BF),
        vm(RT, D, BF),
        vm(RT, DD, BF),
        vm(RT, D, F32),
        vm(RT, D, BF),
        vm(RT, DD, BF),
        vm(MICROS, CHIPS, 16, PK, BF),
        vm(MICROS, CHIPS, 16, PK, BF),
        vm(MICROS, RP, RP, BF),
        pltpu.VMEM(tok.shape, BF),
        vm(2, NZ, NY, NX, CH, 768, BF),
        vm(SLOTS, NZ, 2, CH, 384, BF),
        vm(SLOTS, NZ, 2, CH, 384, BF),
        vm(SLOTS, NZ, CH, 384, BF),
        vm(SLOTS, NZ, CH, 384, BF),
        vm(NZ - 1, CH, C_ALL, BF),
        vm(24, SWAPPED, F32),
        vm(2, CH, 768, F32),
        vm(24, 512, F32),
        vm(MICROS, FULL // EC, EC, jnp.int32),
        vm(8, DD, F32),
        vm(6, 8, DD, F32),
    ]
    sems = [
        sem(11), sem(6), sem(2), sem(1), sem(2), sem(2, 1), sem(2, 9, 3), sem(2, 9, 2), sem(2, 9, 2), sem(2, 9), sem(2, 2, 15), sem(2, 2, 15),
        sem(2, 10), sem(2, 10, 2), sem(2, 10, 2), sem(2, 10, 3), sem(2, 10), sem(2, 6), sem(2, 3, 4),
    ]
    out = pl.pallas_call(
        _mega,
        out_shape=[jax.ShapeDtypeStruct(cot.shape, BF), jax.ShapeDtypeStruct(tok.shape, BF)] + grads,
        in_specs=[ANY] * 13,
        out_specs=[ANY] * 8,
        scratch_shapes=held + scratch + sems,
        compiler_params=pltpu.CompilerParams(collective_id=0, has_side_effects=True, vmem_limit_bytes=VMEM_BYTES),
    )(tok, *raw, cot)
    return out


VMEM_BYTES = 67_000_000


def _hand_over(*refs):
    ins, outs, o_ga, o_gm, o_mask = refs[:8], refs[8:15], refs[15], refs[16], refs[17]
    bufs, vbuf, in_sem, out_sem = refs[18:25], refs[25], refs[26], refs[27]
    parts = ins[0].shape[1] // 4
    pieces = [(0, (m, slice(i * parts, (i + 1) * parts))) for m in range(MICROS) for i in range(4)]
    pieces += [(k, (slice(None),)) for k in range(1, 7)]
    load = pltpu.make_async_copy(ins[7], vbuf, in_sem.at[len(pieces)])
    load.start()
    loads = [pltpu.make_async_copy(ins[k].at[at], bufs[k].at[at], in_sem.at[i]) for i, (k, at) in enumerate(pieces)]
    stores = [pltpu.make_async_copy(bufs[k].at[at], outs[k].at[at], out_sem.at[i]) for i, (k, at) in enumerate(pieces)]
    for c in loads:
        c.start()
    load.wait()
    n = o_ga.shape[0]
    me = lax.axis_index("dp") * 2 + lax.axis_index("fsdp")
    v = vbuf[...]
    for i, o in ((1, o_ga), (3, o_gm)):
        row = jnp.concatenate([v[i : i + 1], v[i + 1 : i + 2]], axis=1)
        turned = pltpu.roll(jnp.broadcast_to(row, (8, D)), D - n * me, 1)
        o[...] = turned[0:1, 0:n].reshape(n)
    o_mask[...] = v[0:1].reshape(DD)
    for c, d in zip(loads, stores):
        c.wait()
        d.start()
    for d in stores:
        d.wait()


def _hand_over_call(n, *arrays):
    V = pl.BlockSpec(memory_space=pltpu.VMEM)
    ANY = pl.BlockSpec(memory_space=pl.ANY)
    like = lambda a: jax.ShapeDtypeStruct(a.shape, a.dtype)
    flat = lambda k: jax.ShapeDtypeStruct((k,), F32)
    return pl.pallas_call(
        _hand_over,
        out_shape=[like(a) for a in arrays[:7]] + [flat(n), flat(n), flat(DD)],
        in_specs=[ANY] * 8,
        out_specs=[ANY] * 7 + [V] * 3,
        scratch_shapes=[pltpu.VMEM(a.shape, a.dtype) for a in arrays]
        + [pltpu.SemaphoreType.DMA((15,)), pltpu.SemaphoreType.DMA((14,))],
        compiler_params=pltpu.CompilerParams(vmem_limit_bytes=VMEM_BYTES),
    )(*arrays)


def per_device_fused(
    tokens, gain_attn, gain_mlp, w_qkv, w_out, w_up, w_down, w_dec, mask_token, clip_lengths, vis_index, pos_index, cotangent,
):
    tok = jnp.transpose(tokens[0], (1, 0, 2))
    made = _mega_call(
        tok, w_qkv, w_out, w_up, w_dec, w_down, gain_attn, gain_mlp, mask_token,
        clip_lengths[0], vis_index[0], pos_index[0], cotangent[0],
    )
    rows_out, returned, g_qkv, g_out, g_up, g_dec, g_down, ga, gm, mask = _hand_over_call(gain_attn.shape[0], *made)
    returned = jnp.transpose(returned, (1, 0, 2))
    return (rows_out[None], returned[None], ga, gm, g_qkv, g_out, g_up, g_down, g_dec, mask)

def solution(mesh):
    in_specs = (
        P("fsdp", None, "dp", None),
        P(("dp", "fsdp")),
        P(("dp", "fsdp")),
        P(("dp", "fsdp"), None),
        P(("dp", "fsdp"), None),
        P(("dp", "fsdp"), None),
        P(("dp", "fsdp"), None),
        P(("dp", "fsdp"), None),
        P(),
        P("fsdp", None, None),
        P("fsdp", None, "dp"),
        P("fsdp", None, "dp"),
        P("fsdp", None, "dp", None),
    )
    out_specs = (
        P("fsdp", None, "dp", None),
        P("fsdp", None, "dp", None),
        P(("dp", "fsdp")),
        P(("dp", "fsdp")),
        P(("dp", "fsdp"), None),
        P(("dp", "fsdp"), None),
        P(("dp", "fsdp"), None),
        P(("dp", "fsdp"), None),
        P(("dp", "fsdp"), None),
        P(),
    )
    body = per_device_fused if mesh.shape["dp"] == CHIPS and mesh.shape["fsdp"] == 2 else per_device
    return jax.shard_map(
        body, mesh=mesh, in_specs=in_specs, out_specs=out_specs, check_vma=False
    )
```
